256 devices in a mesh: seq: 128 (over z, y, x), state: 2 (over core).
Axes of the slice: x: 4, y: 4, z: 8, core: 2. Of those that a mesh axis runs over, the one named last changes fastest.
Arguments:
- inputs: bfloat16 [4, 16384, 2048], P(None, 'seq'), may hold values from -6 to 6
- in_proj: bfloat16 [2048, 2, 1024], P(None, None, 'state'), may hold values from -0.125 to 0.125
- decay_rate: float32 [1024], P('state'), may hold values from 1.2207031e-05 to 0.04
- frequency: float32 [1024], P('state'), may hold values from -3.140625 to 3.140625
- readout: bfloat16 [2, 1024, 2048], P(None, 'state'), may hold values from -0.125 to 0.125
- skip_gain: float32 [2048], P('state'), may hold values from 0.5 to 1.5
Outputs:
- outputs: bfloat16 [4, 16384, 2048], P(None, 'seq', 'state')
The draws below stay inside these ranges and needn't reach their ends.
All inputs are finite; a program needn't handle non-finite values.
Results may differ from the reference program's by a relative error of at most 0.004.
Values may be sent and summed in bfloat16 or wider, within the bound.
A program may use at most 128 MiB of HBM per device.

```python
import math
import jax
import jax.numpy as jnp
from jax import lax

H = 2048
P_SIZE = 1024
SEQS = 4
LENGTH = 16384
N_STATE = 2


def level_of(stream_key, shape, cuts, least, top_value):
    gain = 1.0
    for axis_at, shards_of in cuts:
        draws = jax.random.uniform(jax.random.fold_in(jax.random.fold_in(stream_key, 6), axis_at), (shards_of,), jnp.float32, least / len(cuts), top_value / len(cuts))
        gain = gain * jnp.repeat(jnp.exp(draws), shape[axis_at] // shards_of).reshape((-1,) + (1,) * (len(shape) - 1 - axis_at))
    return gain


def normal_values(rng, extent, scale, reach, pieces=(), kind=jnp.bfloat16):
    array = scale * jax.random.normal(rng, extent, jnp.float32)
    if pieces:
        array = array * level_of(rng, extent, pieces, -0.22, 0.18)
    return jnp.clip(array, -reach, reach).astype(kind)


def setup_inputs(seed: int = 0) -> dict:
    key_list = jax.random.split(jax.random.key(seed), 7)
    return {
        "inputs": normal_values(key_list[0], (SEQS, LENGTH, H), 1.0, 6.0, ((1, 128),)),
        "in_proj": normal_values(key_list[1], (H, 2, P_SIZE), H ** -0.5, 0.125, ((2, 2),)),
        "decay_rate": jnp.clip(jnp.exp(math.log(0.04) - 8.094623 * jax.random.uniform(key_list[2], (P_SIZE,), jnp.float32) ** level_of(key_list[2], (P_SIZE,), ((0, 2),), -0.2, 0.2)), 1.220703143189894e-05, 0.04),
        "frequency": jnp.clip(jax.random.uniform(key_list[3], (P_SIZE,), jnp.float32, -3.140625, 3.140625), -3.140625, 3.140625),
        "readout": normal_values(key_list[4], (2, P_SIZE, H), (2 * P_SIZE) ** -0.5, 0.125, ((1, 2),)),
        "skip_gain": jnp.clip(0.5 + 1.0 * jax.random.uniform(key_list[5], (H,), jnp.float32) ** level_of(key_list[5], (H,), ((0, 2),), -0.2, 0.2), 0.5, 1.5),
    }


def combine(earlier, later):
    return (later[0] * earlier[0] - later[1] * earlier[1], later[0] * earlier[1] + later[1] * earlier[0], later[0] * earlier[2] - later[1] * earlier[3] + later[2], later[0] * earlier[3] + later[1] * earlier[2] + later[3])

def reference(inputs, in_proj, decay_rate, frequency, readout, skip_gain):
    seq_count, seq_length, width = inputs.shape
    group_size = P_SIZE // N_STATE
    flat_input = inputs.reshape(seq_count * seq_length, width)
    summed = jnp.zeros((seq_count * seq_length, width), jnp.float32)
    for group_index in range(N_STATE):
        window = slice(group_index * group_size, (group_index + 1) * group_size)
        in_matrix = in_proj[:, :, window].reshape(width, 2 * group_size)
        drive = jnp.dot(flat_input, in_matrix, preferred_element_type=jnp.float32)
        drive = drive.reshape(seq_count, seq_length, 2 * group_size)
        rates = decay_rate[window]
        angles = frequency[window]
        in_scale = jnp.sqrt(-jnp.expm1(-2.0 * rates))
        modulus = jnp.exp(-rates)
        drive_re = drive[..., :group_size] * in_scale
        drive_im = drive[..., group_size:] * in_scale
        lam_re = jnp.broadcast_to(modulus * jnp.cos(angles), drive_re.shape)
        lam_im = jnp.broadcast_to(modulus * jnp.sin(angles), drive_re.shape)
        states = lax.associative_scan(combine, (lam_re, lam_im, drive_re, drive_im), axis=1)
        packed = jnp.concatenate([states[2], states[3]], axis=-1).astype(jnp.bfloat16)
        packed = packed.reshape(seq_count * seq_length, 2 * group_size)
        out_matrix = readout[:, window, :].reshape(2 * group_size, width)
        summed = summed + jnp.dot(packed, out_matrix, preferred_element_type=jnp.float32)
    result = summed + skip_gain[None, :] * flat_input.astype(jnp.float32)
    return result.astype(jnp.bfloat16).reshape(seq_count, seq_length, width)
```

```python
import functools

import jax
import jax.numpy as jnp
from jax import lax
from jax.experimental import pallas as pl
from jax.experimental.pallas import tpu as pltpu
from jax.sharding import PartitionSpec as P

F32 = jnp.float32
BF16 = jnp.bfloat16
MESH_ID = pl.DeviceIdType.MESH

SEQS = 4
STEPS = 128
ROWS = SEQS * STEPS
WIDTH = 2048
POLES = 512
GROUPS = 2
GP = POLES // GROUPS
SUB = 16
CHUNKS = ROWS // SUB
KC = 512
KN = WIDTH // KC
COLS = 1024
LANES = 128
GT = GP // LANES
OT = COLS // LANES
PLANE = 16
DEPTH = 8
PLANE_ORDER = sorted(range(1, PLANE), key=lambda d: -(min(d % 4, 4 - d % 4) + min(d // 4, 4 - d // 4)))
DEPTH_ORDER = sorted(range(1, DEPTH), key=lambda d: -min(d, DEPTH - d))


def cmul(ar, ai, br, bi):
    return ar * br - ai * bi, ar * bi + ai * br


def kernel(
    x_hbm, w_hbm, dec_ref, frq_ref, r_hbm, skip_ref, out_hbm,
    x_v, w_raw, w_v, r_own, r_sib, drive, ends, excl, packed, packed_sib, acc, out_v,
    plane_buf, depth_buf, lam_tab, pow_tab, dep_tab,
    x_sem, w_sem, r_sem, o_sem, rs_send, rs_recv, pl_send, pl_recv, dp_send, dp_recv, pk_send, pk_recv,
):
    me, core = lax.axis_index("seq"), lax.axis_index("state")
    spot, deep = lax.rem(me, PLANE), lax.div(me, PLANE)
    px, py = lax.rem(spot, 4), lax.div(spot, 4)

    def plane_peer(d):
        spot_to = lax.rem(py + d // 4, 4) * 4 + lax.rem(px + d % 4, 4)
        return (deep * PLANE + spot_to, core), spot_to

    def plane_from(d):
        return lax.rem(py + 4 - d // 4, 4) * 4 + lax.rem(px + 4 - d % 4, 4)

    def depth_peer(d):
        return (lax.rem(deep + d, DEPTH) * PLANE + spot, core)

    sibling = (me, 1 - core)

    x_cps, w_cps = [], [[] for _ in range(GROUPS)]
    for k in range(KN):
        cp = pltpu.make_async_copy(x_hbm.at[:, pl.ds(KC * k, KC)], x_v.at[:, pl.ds(KC * k, KC)], x_sem.at[k])
        cp.start()
        x_cps.append(cp)
        cp = pltpu.make_async_copy(w_hbm.at[pl.ds(KC * k, KC), :, pl.ds(0, GP)], w_raw.at[0, k], w_sem.at[0, k])
        cp.start()
        w_cps[0].append(cp)
    for g in range(1, GROUPS):
        for k in range(KN):
            cp = pltpu.make_async_copy(w_hbm.at[pl.ds(KC * k, KC), :, pl.ds(GP * g, GP)], w_raw.at[g, k], w_sem.at[g, k])
            cp.start()
            w_cps[g].append(cp)
    my_cols = pl.multiple_of(core * COLS, COLS)
    sib_cols = pl.multiple_of((1 - core) * COLS, COLS)
    r_cps = []
    for g in range(GROUPS):
        for c in range(2):
            cp = pltpu.make_async_copy(
                r_hbm.at[c, pl.ds(GP * g, GP), pl.ds(my_cols, COLS)], r_own.at[g, pl.ds(GP * c, GP)], r_sem.at[g, c]
            )
            cp.start()
            r_cps.append(cp)

    barrier = pltpu.get_barrier_semaphore()
    for d in DEPTH_ORDER:
        pl.semaphore_signal(barrier, inc=1, device_id=depth_peer(d), device_id_type=MESH_ID)
    for d in PLANE_ORDER:
        pl.semaphore_signal(barrier, inc=1, device_id=plane_peer(d)[0], device_id_type=MESH_ID)
    pl.semaphore_signal(barrier, inc=1, device_id=sibling, device_id_type=MESH_ID)

    dec, frq = dec_ref[...], frq_ref[...]
    mod = jnp.exp(-dec)
    sq = dec * dec
    sinh = dec * (1.0 + sq / 6.0 * (1.0 + sq / 20.0 * (1.0 + sq / 42.0 * (1.0 + sq / 72.0))))
    gam = jnp.sqrt(2.0 * mod * sinh)
    base = (mod * jnp.cos(frq), mod * jnp.sin(frq))
    powers = [None, base]
    for n in range(2, SUB + 1):
        half = powers[n // 2]
        full = cmul(*half, *half)
        powers.append(cmul(*full, *base) if n % 2 else full)
    for n in range(SUB):
        pow_tab[0, pl.ds(n, 1), :] = powers[n + 1][0]
        pow_tab[1, pl.ds(n, 1), :] = powers[n + 1][1]
    one = (jnp.ones_like(dec), jnp.zeros_like(dec))
    subs = [one, powers[SUB]]
    for n in range(2, 9):
        subs.append(cmul(*subs[n // 2], *subs[n - n // 2]))
    sub_re = jnp.concatenate([p[0] for p in subs[:8]], axis=0)
    sub_im = jnp.concatenate([p[1] for p in subs[:8]], axis=0)
    lams = [one, subs[8]]
    for n in range(2, PLANE + 1):
        lams.append(cmul(*lams[n // 2], *lams[n - n // 2]))
    for n in range(PLANE):
        lam_tab[0, pl.ds(n, 1), :] = lams[n][0]
        lam_tab[1, pl.ds(n, 1), :] = lams[n][1]
    lead = lams[PLANE]
    here = (lam_tab[0, pl.ds(spot, 1), :], lam_tab[1, pl.ds(spot, 1), :])
    weight = (jnp.zeros_like(dec), jnp.zeros_like(dec))
    for n in range(DEPTH - 1, -1, -1):
        longer = cmul(*weight, *lead)
        first = deep - 1 == n
        weight = tuple(jnp.where(first, h, w) for h, w in zip(here, longer))
        dep_tab[0, pl.ds(n, 1), :] = weight[0]
        dep_tab[1, pl.ds(n, 1), :] = weight[1]

    step_of = lax.rem(lax.broadcasted_iota(jnp.int32, (CHUNKS, GP), 0), 8)
    sign = jnp.where(lax.broadcasted_iota(jnp.int32, (8, GP), 0) < 4, -1.0, 1.0)

    def weighted(parts, tab, order, lanes):
        along = jnp.zeros((8, GP), F32)
        across = jnp.zeros((8, GP), F32)
        for n, part in enumerate(parts):
            along = along + tab[0, pl.ds(order[n], 1), lanes] * part
            across = across + tab[1, pl.ds(order[n], 1), lanes] * part
        return along + sign * pltpu.roll(across, 4, 0)

    plane_cps, depth_cps, pack_cps, rs_cps = [[] for _ in range(GROUPS)], [[] for _ in range(GROUPS)], [], []

    for k in range(KN):
        x_cps[k].wait()
    for g in range(GROUPS):
        lanes = pl.ds(GP * g, GP)
        for k in range(KN):
            w_cps[g][k].wait()

            def turn(n, carry):
                for u in range(4):
                    at = pl.multiple_of(n * 64 + u * 16, 16)
                    both = jnp.swapaxes(w_raw[g, k, pl.ds(at, 16)], 0, 1)
                    w_v[pl.ds(KC * k + at, 16), pl.ds(0, GP)] = both[0]
                    w_v[pl.ds(KC * k + at, 16), pl.ds(GP, GP)] = both[1]
                return carry

            lax.fori_loop(0, KC // 64, turn, 0)
        driven = jnp.dot(x_v[...], w_v[...], preferred_element_type=F32)
        for t in range(2 * GT):
            drive[g, t] = driven[:, LANES * t : LANES * (t + 1)]

        lr, li = base[0][:, GP * g : GP * (g + 1)], base[1][:, GP * g : GP * (g + 1)]
        gg = gam[:, GP * g : GP * (g + 1)]
        sr = jnp.zeros((CHUNKS, GP), F32)
        si = jnp.zeros((CHUNKS, GP), F32)
        for i in range(SUB):
            tiles = [drive[g, t, pl.ds(i, CHUNKS, stride=SUB), :] for t in range(2 * GT)]
            nr = lr * sr - li * si + gg * jnp.concatenate(tiles[:GT], axis=1)
            ni = lr * si + li * sr + gg * jnp.concatenate(tiles[GT:], axis=1)
            sr, si = nr, ni
            ends[g, pl.ds(CHUNKS * i, CHUNKS), pl.ds(0, GP)] = sr
            ends[g, pl.ds(CHUNKS * i, CHUNKS), pl.ds(GP, GP)] = si
        for d in (1, 2, 4):
            mr = jnp.where(step_of >= d, subs[d][0][:, GP * g : GP * (g + 1)], 0.0)
            mi = jnp.where(step_of >= d, subs[d][1][:, GP * g : GP * (g + 1)], 0.0)
            tr, ti = pltpu.roll(sr, d, 0), pltpu.roll(si, d, 0)
            sr, si = sr + mr * tr - mi * ti, si + mr * ti + mi * tr
        for s in range(SEQS):
            plane_buf[g, spot, pl.ds(s, 1), :] = sr[8 * s + 7 : 8 * s + 8]
            plane_buf[g, spot, pl.ds(4 + s, 1), :] = si[8 * s + 7 : 8 * s + 8]
        excl[g, 0] = jnp.where(step_of >= 1, pltpu.roll(sr, 1, 0), 0.0)
        excl[g, 1] = jnp.where(step_of >= 1, pltpu.roll(si, 1, 0), 0.0)

        if g == 0:
            pl.semaphore_wait(barrier, DEPTH + PLANE - 1)
        for d in PLANE_ORDER:
            cp = pltpu.make_async_remote_copy(
                src_ref=plane_buf.at[g, spot], dst_ref=plane_buf.at[g, spot], send_sem=pl_send.at[g, d],
                recv_sem=pl_recv.at[g, d], device_id=plane_peer(d)[0], device_id_type=MESH_ID,
            )
            cp.start()
            plane_cps[g].append(cp)
        if g == GROUPS - 1:
            for h in range(GROUPS):
                for c in range(2):
                    cp = pltpu.make_async_remote_copy(
                        src_ref=r_hbm.at[c, pl.ds(GP * h, GP), pl.ds(sib_cols, COLS)],
                        dst_ref=r_sib.at[h, pl.ds(GP * c, GP)], send_sem=rs_send.at[h, c],
                        recv_sem=rs_recv.at[h, c], device_id=sibling, device_id_type=MESH_ID,
                    )
                    cp.start()
                    rs_cps.append(cp)

    entering = []
    for g in range(GROUPS):
        lanes = pl.ds(GP * g, GP)
        for cp in plane_cps[g]:
            cp.wait_recv()
        parts = [plane_buf[g, n] for n in range(PLANE)]
        depth_buf[g, deep] = weighted(parts, lam_tab, [PLANE - 1 - n for n in range(PLANE)], lanes)
        for d in DEPTH_ORDER:
            cp = pltpu.make_async_remote_copy(
                src_ref=depth_buf.at[g, deep], dst_ref=depth_buf.at[g, deep], send_sem=dp_send.at[g, d],
                recv_sem=dp_recv.at[g, d], device_id=depth_peer(d), device_id_type=MESH_ID,
            )
            cp.start()
            depth_cps[g].append(cp)
        lam_re, lam_im = lam_tab[0, pl.ds(1, 1), lanes], lam_tab[1, pl.ds(1, 1), lanes] * sign
        before = jnp.zeros((8, GP), F32)
        for n in range(PLANE - 1):
            longer = lam_re * before + lam_im * pltpu.roll(before, 4, 0) + parts[n]
            before = jnp.where(n < spot, longer, before)
        entering.append(before)
    for cp in r_cps:
        cp.wait()
    for cp in rs_cps:
        cp.wait_recv()

    skip = skip_ref[...]
    for g in range(GROUPS):
        lanes = pl.ds(GP * g, GP)
        for cp in depth_cps[g]:
            cp.wait_recv()
        come = entering[g] + weighted([depth_buf[g, n] for n in range(DEPTH)], dep_tab, list(range(DEPTH)), lanes)
        cr = jnp.concatenate([jnp.broadcast_to(come[s : s + 1], (8, GP)) for s in range(SEQS)], axis=0)
        ci = jnp.concatenate([jnp.broadcast_to(come[4 + s : 5 + s], (8, GP)) for s in range(SEQS)], axis=0)
        qr = jnp.concatenate([sub_re[:, GP * g : GP * (g + 1)]] * SEQS, axis=0)
        qi = jnp.concatenate([sub_im[:, GP * g : GP * (g + 1)]] * SEQS, axis=0)
        tr = excl[g, 0] + qr * cr - qi * ci
        ti = excl[g, 1] + qr * ci + qi * cr
        for i in range(SUB):
            ar, ai = pow_tab[0, pl.ds(i, 1), lanes], pow_tab[1, pl.ds(i, 1), lanes]
            rows = pl.ds(CHUNKS * i, CHUNKS)
            packed[g, rows, pl.ds(0, GP)] = (ends[g, rows, pl.ds(0, GP)] + ar * tr - ai * ti).astype(BF16)
            packed[g, rows, pl.ds(GP, GP)] = (ends[g, rows, pl.ds(GP, GP)] + ar * ti + ai * tr).astype(BF16)
        cp = pltpu.make_async_remote_copy(
            src_ref=packed.at[g], dst_ref=packed_sib.at[g], send_sem=pk_send.at[g], recv_sem=pk_recv.at[g],
            device_id=sibling, device_id_type=MESH_ID,
        )
        cp.start()
        pack_cps.append(cp)
        part = jnp.dot(packed[g], r_own[g], preferred_element_type=F32)
        for t in range(OT):
            tile = part[:, LANES * t : LANES * (t + 1)]
            acc[t] = tile if g == 0 else acc[t] + tile
        cp.wait_recv()
        if g < GROUPS - 1:
            part = jnp.dot(packed_sib[g], r_sib[g], preferred_element_type=F32)
            for t in range(OT):
                acc[t] += part[:, LANES * t : LANES * (t + 1)]
    out_cps = []
    last = GROUPS - 1
    CN = 256
    for c in range(COLS // CN):
        part = jnp.dot(packed_sib[last], r_sib[last, :, pl.ds(CN * c, CN)], preferred_element_type=F32)
        of_chunk = range(CN // LANES * c, CN // LANES * (c + 1))
        for n, t in enumerate(of_chunk):
            acc[t] += part[:, LANES * n : LANES * (n + 1)]
        gain = skip[:, CN * c : CN * (c + 1)]
        from_col = pl.multiple_of(core * COLS + CN * c, CN)
        for q in range(CHUNKS):
            straight = x_v[pl.ds(SUB * q, SUB), pl.ds(from_col, CN)].astype(F32) * gain
            summed = jnp.concatenate([acc[t, pl.ds(q, SUB, stride=CHUNKS), :] for t in of_chunk], axis=1)
            out_v[pl.ds(SUB * q, SUB), pl.ds(CN * c, CN)] = (summed + straight).astype(BF16)
        cp = pltpu.make_async_copy(out_v.at[:, pl.ds(CN * c, CN)], out_hbm.at[:, pl.ds(CN * c, CN)], o_sem.at[c])
        cp.start()
        out_cps.append(cp)
    for cp in out_cps:
        cp.wait()
    for g in range(GROUPS):
        for cp in plane_cps[g] + depth_cps[g]:
            cp.wait_send()
    for cp in pack_cps + rs_cps:
        cp.wait_send()


def local(inputs, in_proj, decay_rate, frequency, readout, skip_gain):
    vmem = pl.BlockSpec(memory_space=pltpu.VMEM)
    hbm = pl.BlockSpec(memory_space=pl.ANY)
    dma = pltpu.SemaphoreType.DMA
    out = pl.pallas_call(
        kernel,
        out_shape=jax.ShapeDtypeStruct((ROWS, COLS), BF16),
        in_specs=[hbm, hbm, vmem, vmem, hbm, vmem],
        out_specs=hbm,
        scratch_shapes=[
            pltpu.VMEM((ROWS, WIDTH), BF16),
            pltpu.VMEM((GROUPS, KN, KC, 2, GP), BF16),
            pltpu.VMEM((WIDTH, 2 * GP), BF16),
            pltpu.VMEM((GROUPS, 2 * GP, COLS), BF16),
            pltpu.VMEM((GROUPS, 2 * GP, COLS), BF16),
            pltpu.VMEM((GROUPS, 2 * GT, ROWS, LANES), F32),
            pltpu.VMEM((GROUPS, ROWS, 2 * GP), F32),
            pltpu.VMEM((GROUPS, 2, CHUNKS, GP), F32),
            pltpu.VMEM((GROUPS, ROWS, 2 * GP), BF16),
            pltpu.VMEM((GROUPS, ROWS, 2 * GP), BF16),
            pltpu.VMEM((OT, ROWS, LANES), F32),
            pltpu.VMEM((ROWS, COLS), BF16),
            pltpu.VMEM((GROUPS, PLANE, 8, GP), F32),
            pltpu.VMEM((GROUPS, DEPTH, 8, GP), F32),
            pltpu.VMEM((2, PLANE, POLES), F32),
            pltpu.VMEM((2, SUB, POLES), F32),
            pltpu.VMEM((2, DEPTH, POLES), F32),
            dma((KN,)),
            dma((GROUPS, KN)),
            dma((GROUPS, 2)),
            dma((4,)),
            dma((GROUPS, 2)),
            dma((GROUPS, 2)),
            dma((GROUPS, PLANE)),
            dma((GROUPS, PLANE)),
            dma((GROUPS, DEPTH)),
            dma((GROUPS, DEPTH)),
            dma((GROUPS,)),
            dma((GROUPS,)),
        ],
        compiler_params=pltpu.CompilerParams(
            collective_id=0, has_side_effects=True, vmem_limit_bytes=48 << 20
        ),
    )(
        inputs.reshape(ROWS, WIDTH), in_proj, decay_rate.reshape(1, POLES), frequency.reshape(1, POLES),
        readout, skip_gain.reshape(1, COLS),
    )
    return out.reshape(SEQS, STEPS, COLS)


def solution(mesh):
    in_specs = (
        P(None, "seq", None),
        P(None, None, "state"),
        P("state"),
        P("state"),
        P(None, "state", None),
        P("state"),
    )
    out_specs = P(None, "seq", "state")
    return jax.shard_map(local, mesh=mesh, in_specs=in_specs, out_specs=out_specs, check_vma=False)
```

```python
import functools

import jax
import jax.numpy as jnp
from jax import lax
from jax.experimental import pallas as pl
from jax.experimental.pallas import tpu as pltpu
from jax.sharding import PartitionSpec as P

F32 = jnp.float32
BF16 = jnp.bfloat16
MESH_ID = pl.DeviceIdType.MESH

SEQS = 4
STEPS = 128
ROWS = SEQS * STEPS
WIDTH = 2048
POLES = 512
GROUPS = 2
GP = POLES // GROUPS
SUB = 16
CHUNKS = ROWS // SUB
KC = 512
KN = WIDTH // KC
COLS = 1024
LANES = 128
GT = GP // LANES
HALVES = 2
HALF = ROWS // HALVES
CN = 256
PLANE = 16
DEPTH = 8
PLANE_ORDER = sorted(range(1, PLANE), key=lambda d: -(min(d % 4, 4 - d % 4) + min(d // 4, 4 - d // 4)))
DEPTH_ORDER = sorted(range(1, DEPTH), key=lambda d: -min(d, DEPTH - d))


def cmul(ar, ai, br, bi):
    return ar * br - ai * bi, ar * bi + ai * br


def kernel(
    x_hbm, w_hbm, dec_hbm, frq_hbm, r_hbm, skip_hbm, out_hbm,
    dec_ref, frq_ref, skip_ref, x_v, w_raw, w_v, r_own, r_sib, drive, enter, excl, packed, packed_sib, acc, out_v,
    plane_buf, depth_buf, lam_tab, pow_tab, dep_tab,
    s_sem, x_sem, w_sem, r_sem, o_sem, rs_send, rs_recv, pl_send, pl_recv, dp_send, dp_recv, pk_send, pk_recv, ready_sem,
):
    me, core = lax.axis_index("seq"), lax.axis_index("state")
    spot, deep = lax.rem(me, PLANE), lax.div(me, PLANE)
    px, py = lax.rem(spot, 4), lax.div(spot, 4)

    def plane_peer(d):
        spot_to = lax.rem(py + d // 4, 4) * 4 + lax.rem(px + d % 4, 4)
        return (deep * PLANE + spot_to, core), spot_to

    def depth_peer(d):
        return ((deep + d) * PLANE + spot, core)

    sibling = (me, 1 - core)

    barrier = pltpu.get_barrier_semaphore()
    for d in PLANE_ORDER:
        pl.semaphore_signal(barrier, inc=1, device_id=plane_peer(d)[0], device_id_type=MESH_ID)
    pl.semaphore_signal(barrier, inc=1, device_id=sibling, device_id_type=MESH_ID)

    def after(d, act):
        pl.when(deep + d < DEPTH)(act)

    def before(d, act):
        pl.when(deep - d >= 0)(act)

    def greet(d):
        pl.semaphore_signal(barrier, inc=1, device_id=depth_peer(d), device_id_type=MESH_ID)

    def answer(d):
        pl.semaphore_signal(ready_sem, inc=1, device_id=depth_peer(-d), device_id_type=MESH_ID)

    for d in DEPTH_ORDER:
        after(d, functools.partial(greet, d))

    small = [
        pltpu.make_async_copy(src, dst, s_sem.at[n])
        for n, (src, dst) in enumerate(((dec_hbm, dec_ref), (frq_hbm, frq_ref), (skip_hbm, skip_ref)))
    ]
    for cp in small:
        cp.start()
    x_cps, w_cps = [], [[] for _ in range(GROUPS)]
    for k in range(KN):
        cp = pltpu.make_async_copy(x_hbm.at[:, pl.ds(KC * k, KC)], x_v.at[:, pl.ds(KC * k, KC)], x_sem.at[k])
        cp.start()
        x_cps.append(cp)
        cp = pltpu.make_async_copy(w_hbm.at[pl.ds(KC * k, KC), :, pl.ds(0, GP)], w_raw.at[0, k], w_sem.at[0, k])
        cp.start()
        w_cps[0].append(cp)
    for g in range(1, GROUPS):
        for k in range(KN):
            cp = pltpu.make_async_copy(w_hbm.at[pl.ds(KC * k, KC), :, pl.ds(GP * g, GP)], w_raw.at[g, k], w_sem.at[g, k])
            cp.start()
            w_cps[g].append(cp)
    my_cols = pl.multiple_of(core * COLS, COLS)
    sib_cols = pl.multiple_of((1 - core) * COLS, COLS)
    r_cps = []
    for g in range(GROUPS):
        for c in range(2):
            cp = pltpu.make_async_copy(
                r_hbm.at[c, pl.ds(GP * g, GP), pl.ds(my_cols, COLS)], r_own.at[g, pl.ds(GP * c, GP)], r_sem.at[g, c]
            )
            cp.start()
            r_cps.append(cp)

    depth_buf[...] = jnp.zeros_like(depth_buf)
    for cp in small:
        cp.wait()
    dec, frq = dec_ref[...], frq_ref[...]
    mod = jnp.exp(-dec)
    sq = dec * dec
    sinh = dec * (1.0 + sq / 6.0 * (1.0 + sq / 20.0 * (1.0 + sq / 42.0 * (1.0 + sq / 72.0))))
    gam = jnp.sqrt(2.0 * mod * sinh)
    base = (mod * jnp.cos(frq), mod * jnp.sin(frq))
    powers = [None, base]
    for n in range(2, SUB + 1):
        half = powers[n // 2]
        full = cmul(*half, *half)
        powers.append(cmul(*full, *base) if n % 2 else full)
    for n in range(SUB):
        pow_tab[0, pl.ds(n, 1), :] = powers[n + 1][0]
        pow_tab[1, pl.ds(n, 1), :] = powers[n + 1][1]
    one = (jnp.ones_like(dec), jnp.zeros_like(dec))
    subs = [one, powers[SUB]]
    for n in range(2, 9):
        subs.append(cmul(*subs[n // 2], *subs[n - n // 2]))
    sub_re = jnp.concatenate([p[0] for p in subs[:8]], axis=0)
    sub_im = jnp.concatenate([p[1] for p in subs[:8]], axis=0)
    lams = [one, subs[8]]
    for n in range(2, PLANE + 1):
        lams.append(cmul(*lams[n // 2], *lams[n - n // 2]))
    for n in range(PLANE):
        lam_tab[0, pl.ds(n, 1), :] = lams[n][0]
        lam_tab[1, pl.ds(n, 1), :] = lams[n][1]
    lead = lams[PLANE]
    here = (lam_tab[0, pl.ds(spot, 1), :], lam_tab[1, pl.ds(spot, 1), :])
    weight = (jnp.zeros_like(dec), jnp.zeros_like(dec))
    for n in range(DEPTH - 1, -1, -1):
        longer = cmul(*weight, *lead)
        first = deep - 1 == n
        weight = tuple(jnp.where(first, h, w) for h, w in zip(here, longer))
        dep_tab[0, pl.ds(n, 1), :] = weight[0]
        dep_tab[1, pl.ds(n, 1), :] = weight[1]

    step_of = lax.rem(lax.broadcasted_iota(jnp.int32, (CHUNKS, GP), 0), 8)
    sign = jnp.where(lax.broadcasted_iota(jnp.int32, (8, GP), 0) < 4, -1.0, 1.0)

    def weighted(parts, tab, order, lanes):
        along = jnp.zeros((8, GP), F32)
        across = jnp.zeros((8, GP), F32)
        for n, part in enumerate(parts):
            along = along + tab[0, pl.ds(order[n], 1), lanes] * part
            across = across + tab[1, pl.ds(order[n], 1), lanes] * part
        return along + sign * pltpu.roll(across, 4, 0)

    plane_cps, depth_cps, pack_cps, rs_cps = [[] for _ in range(GROUPS)], [[] for _ in range(GROUPS)], [], []

    for k in range(KN):
        x_cps[k].wait()
    for g in range(GROUPS):
        lanes = pl.ds(GP * g, GP)
        for k in range(KN):
            w_cps[g][k].wait()

            def turn(n, carry):
                for u in range(4):
                    at = pl.multiple_of(n * 64 + u * 16, 16)
                    both = jnp.swapaxes(w_raw[g, k, pl.ds(at, 16)], 0, 1)
                    w_v[pl.ds(KC * k + at, 16), pl.ds(0, GP)] = both[0]
                    w_v[pl.ds(KC * k + at, 16), pl.ds(GP, GP)] = both[1]
                return carry

            lax.fori_loop(0, KC // 64, turn, 0)
        driven = jnp.dot(x_v[...], w_v[...], preferred_element_type=F32)
        for t in range(2 * GT):
            drive[g, t] = driven[:, LANES * t : LANES * (t + 1)]

        lr, li = base[0][:, GP * g : GP * (g + 1)], base[1][:, GP * g : GP * (g + 1)]
        gg = gam[:, GP * g : GP * (g + 1)]
        sr = jnp.zeros((CHUNKS, GP), F32)
        si = jnp.zeros((CHUNKS, GP), F32)
        for i in range(SUB):
            tiles = [drive[g, t, pl.ds(i, CHUNKS, stride=SUB), :] for t in range(2 * GT)]
            nr = lr * sr - li * si + gg * jnp.concatenate(tiles[:GT], axis=1)
            ni = lr * si + li * sr + gg * jnp.concatenate(tiles[GT:], axis=1)
            sr, si = nr, ni
            for t in range(GT):
                drive[g, t, pl.ds(i, CHUNKS, stride=SUB), :] = sr[:, LANES * t : LANES * (t + 1)]
                drive[g, GT + t, pl.ds(i, CHUNKS, stride=SUB), :] = si[:, LANES * t : LANES * (t + 1)]
        for d in (1, 2, 4):
            mr = jnp.where(step_of >= d, subs[d][0][:, GP * g : GP * (g + 1)], 0.0)
            mi = jnp.where(step_of >= d, subs[d][1][:, GP * g : GP * (g + 1)], 0.0)
            tr, ti = pltpu.roll(sr, d, 0), pltpu.roll(si, d, 0)
            sr, si = sr + mr * tr - mi * ti, si + mr * ti + mi * tr
        last = [v[8 * s + 7 : 8 * s + 8] for v in (sr, si) for s in range(SEQS)]
        last = jnp.concatenate(last, axis=0)
        tiles = [last[:, LANES * t : LANES * (t + 1)] for t in range(GT)]
        plane_buf[g, spot] = jnp.concatenate(tiles, axis=0)
        excl[g, 0] = jnp.where(step_of >= 1, pltpu.roll(sr, 1, 0), 0.0)
        excl[g, 1] = jnp.where(step_of >= 1, pltpu.roll(si, 1, 0), 0.0)

        if g == 0:
            pl.semaphore_wait(barrier, PLANE + deep)
            for d in DEPTH_ORDER:
                before(d, functools.partial(answer, d))
        for d in PLANE_ORDER:
            cp = pltpu.make_async_remote_copy(
                src_ref=plane_buf.at[g, spot], dst_ref=plane_buf.at[g, spot], send_sem=pl_send.at[g, d],
                recv_sem=pl_recv.at[g, d], device_id=plane_peer(d)[0], device_id_type=MESH_ID,
            )
            cp.start()
            plane_cps[g].append(cp)
        if g == 0:
            for h in range(GROUPS):
                for c in range(2):
                    cp = pltpu.make_async_remote_copy(
                        src_ref=r_hbm.at[c, pl.ds(GP * h, GP), pl.ds(sib_cols, COLS)],
                        dst_ref=r_sib.at[h, pl.ds(GP * c, GP)], send_sem=rs_send.at[h, c],
                        recv_sem=rs_recv.at[h, c], device_id=sibling, device_id_type=MESH_ID,
                    )
                    cp.start()
                    rs_cps.append(cp)

    entering = []
    for g in range(GROUPS):
        lanes = pl.ds(GP * g, GP)
        for cp in plane_cps[g]:
            cp.wait_recv()
        parts = [plane_buf[g, n].astype(F32) for n in range(PLANE)]
        parts = [jnp.concatenate([p[8 * t : 8 * (t + 1)] for t in range(GT)], axis=1) for p in parts]
        depth_buf[g, deep] = weighted(parts, lam_tab, [PLANE - 1 - n for n in range(PLANE)], lanes)
        if g == 0:

            @pl.when(deep < DEPTH - 1)
            def _():
                pl.semaphore_wait(ready_sem, DEPTH - 1 - deep)

        for d in DEPTH_ORDER:
            cp = pltpu.make_async_remote_copy(
                src_ref=depth_buf.at[g, deep], dst_ref=depth_buf.at[g, deep], send_sem=dp_send.at[g, d],
                recv_sem=dp_recv.at[g, d], device_id=depth_peer(d), device_id_type=MESH_ID,
            )
            after(d, cp.start)
            depth_cps[g].append((d, cp))
        lam_re, lam_im = lam_tab[0, pl.ds(1, 1), lanes], lam_tab[1, pl.ds(1, 1), lanes] * sign
        pre = jnp.zeros((8, GP), F32)
        for n in range(PLANE - 1):
            longer = lam_re * pre + lam_im * pltpu.roll(pre, 4, 0) + parts[n]
            pre = jnp.where(n < spot, longer, pre)
        entering.append(pre)
    for cp in r_cps:
        cp.wait()
    for cp in rs_cps:
        cp.wait_recv()

    skip = skip_ref[...]
    for g in range(GROUPS):
        lanes = pl.ds(GP * g, GP)
        for d, cp in depth_cps[g]:
            before(d, cp.wait_recv)
        come = entering[g] + weighted([depth_buf[g, n] for n in range(DEPTH)], dep_tab, list(range(DEPTH)), lanes)
        cr = jnp.concatenate([jnp.broadcast_to(come[s : s + 1], (8, GP)) for s in range(SEQS)], axis=0)
        ci = jnp.concatenate([jnp.broadcast_to(come[4 + s : 5 + s], (8, GP)) for s in range(SEQS)], axis=0)
        qr = jnp.concatenate([sub_re[:, GP * g : GP * (g + 1)]] * SEQS, axis=0)
        qi = jnp.concatenate([sub_im[:, GP * g : GP * (g + 1)]] * SEQS, axis=0)
        tr = excl[g, 0] + qr * cr - qi * ci
        ti = excl[g, 1] + qr * ci + qi * cr
        enter[g, 0], enter[g, 1] = tr, ti
        ar, ai = pow_tab[0, :, lanes], pow_tab[1, :, lanes]
        for h in range(HALVES):
            for q in range(CHUNKS // HALVES * h, CHUNKS // HALVES * (h + 1)):
                rows = pl.ds(SUB * q, SUB)
                br, bi = enter[g, 0, pl.ds(q, 1), :], enter[g, 1, pl.ds(q, 1), :]
                er = jnp.concatenate([drive[g, t, rows, :] for t in range(GT)], axis=1)
                ei = jnp.concatenate([drive[g, GT + t, rows, :] for t in range(GT)], axis=1)
                packed[g, rows, pl.ds(0, GP)] = (er + ar * br - ai * bi).astype(BF16)
                packed[g, rows, pl.ds(GP, GP)] = (ei + ar * bi + ai * br).astype(BF16)
            rows = pl.ds(HALF * h, HALF)
            cp = pltpu.make_async_remote_copy(
                src_ref=packed.at[g, rows], dst_ref=packed_sib.at[g, rows], send_sem=pk_send.at[g, h],
                recv_sem=pk_recv.at[g, h], device_id=sibling, device_id_type=MESH_ID,
            )
            cp.start()
            pack_cps.append(cp)
        part = jnp.dot(packed[g], r_own[g], preferred_element_type=F32)
        if g == 0:
            straight = x_v[:, pl.ds(my_cols, COLS)].astype(F32) * skip
            acc[...] = part + straight
        else:
            acc[...] += part
        if g < GROUPS - 1:
            for cp in pack_cps[-HALVES:]:
                cp.wait_recv()
            acc[...] += jnp.dot(packed_sib[g], r_sib[g], preferred_element_type=F32)
    out_cps = []
    last = GROUPS - 1
    for h in range(HALVES):
        pack_cps[h - HALVES].wait_recv()
        rows = pl.ds(HALF * h, HALF)
        for c in range(COLS // CN):
            cols = pl.ds(CN * c, CN)
            part = jnp.dot(packed_sib[last, rows, :], r_sib[last, :, cols], preferred_element_type=F32)
            out_v[rows, cols] = (acc[rows, cols] + part).astype(BF16)
        cp = pltpu.make_async_copy(out_v.at[rows], out_hbm.at[rows], o_sem.at[h])
        cp.start()
        out_cps.append(cp)
    for cp in out_cps:
        cp.wait()
    for g in range(GROUPS):
        for cp in plane_cps[g]:
            cp.wait_send()
        for d, cp in depth_cps[g]:
            after(d, cp.wait_send)
    for cp in pack_cps + rs_cps:
        cp.wait_send()


def local(inputs, in_proj, decay_rate, frequency, readout, skip_gain):
    hbm = pl.BlockSpec(memory_space=pltpu.HBM)
    dma = pltpu.SemaphoreType.DMA
    out = pl.pallas_call(
        kernel,
        out_shape=jax.ShapeDtypeStruct((ROWS, COLS), BF16),
        in_specs=[hbm] * 6,
        out_specs=pl.BlockSpec(memory_space=pl.ANY),
        scratch_shapes=[
            pltpu.VMEM((1, POLES), F32),
            pltpu.VMEM((1, POLES), F32),
            pltpu.VMEM((1, COLS), F32),
            pltpu.VMEM((ROWS, WIDTH), BF16),
            pltpu.VMEM((GROUPS, KN, KC, 2, GP), BF16),
            pltpu.VMEM((WIDTH, 2 * GP), BF16),
            pltpu.VMEM((GROUPS, 2 * GP, COLS), BF16),
            pltpu.VMEM((GROUPS, 2 * GP, COLS), BF16),
            pltpu.VMEM((GROUPS, 2 * GT, ROWS, LANES), F32),
            pltpu.VMEM((GROUPS, 2, CHUNKS, GP), F32),
            pltpu.VMEM((GROUPS, 2, CHUNKS, GP), F32),
            pltpu.VMEM((GROUPS, ROWS, 2 * GP), BF16),
            pltpu.VMEM((GROUPS, ROWS, 2 * GP), BF16),
            pltpu.VMEM((ROWS, COLS), F32),
            pltpu.VMEM((ROWS, COLS), BF16),
            pltpu.VMEM((GROUPS, PLANE, 8 * GT, LANES), F32),
            pltpu.VMEM((GROUPS, DEPTH, 8, GP), F32),
            pltpu.VMEM((2, PLANE, POLES), F32),
            pltpu.VMEM((2, SUB, POLES), F32),
            pltpu.VMEM((2, DEPTH, POLES), F32),
            dma((3,)),
            dma((KN,)),
            dma((GROUPS, KN)),
            dma((GROUPS, 2)),
            dma((4,)),
            dma((GROUPS, 2)),
            dma((GROUPS, 2)),
            dma((GROUPS, PLANE)),
            dma((GROUPS, PLANE)),
            dma((GROUPS, DEPTH)),
            dma((GROUPS, DEPTH)),
            dma((GROUPS, HALVES)),
            dma((GROUPS, HALVES)),
            pltpu.SemaphoreType.REGULAR,
        ],
        compiler_params=pltpu.CompilerParams(
            collective_id=0, has_side_effects=True, vmem_limit_bytes=64 << 20
        ),
    )(
        inputs.reshape(ROWS, WIDTH), in_proj, decay_rate.reshape(1, POLES), frequency.reshape(1, POLES),
        readout, skip_gain.reshape(1, COLS),
    )
    return out.reshape(SEQS, STEPS, COLS)


def solution(mesh):
    in_specs = (
        P(None, "seq", None),
        P(None, None, "state"),
        P("state"),
        P("state"),
        P(None, "state", None),
        P("state"),
    )
    out_specs = P(None, "seq", "state")
    return jax.shard_map(local, mesh=mesh, in_specs=in_specs, out_specs=out_specs, check_vma=False)
```

```python
import functools

import jax
import jax.numpy as jnp
from jax import lax
from jax.experimental import pallas as pl
from jax.experimental.pallas import tpu as pltpu
from jax.sharding import PartitionSpec as P

F32 = jnp.float32
BF16 = jnp.bfloat16
MESH_ID = pl.DeviceIdType.MESH

SEQS = 4
STEPS = 128
ROWS = SEQS * STEPS
WIDTH = 2048
POLES = 512
GROUPS = 1
GP = POLES // GROUPS
SUB = 16
CHUNKS = ROWS // SUB
KC = 512
KN = WIDTH // KC
AHEAD = 2
PITCH = 17
COLS = 1024
LANES = 128
GT = GP // LANES
HALVES = 2
HALF = ROWS // HALVES
CN = 256
PLANE = 16
DEPTH = 8
PLANE_ORDER = sorted(range(1, PLANE), key=lambda d: -(min(d % 4, 4 - d % 4) + min(d // 4, 4 - d // 4)))
DEPTH_ORDER = sorted(range(1, DEPTH), key=lambda d: -min(d, DEPTH - d))


def cmul(ar, ai, br, bi):
    return ar * br - ai * bi, ar * bi + ai * br


def kernel(
    x_hbm, w_hbm, dec_hbm, frq_hbm, r_hbm, skip_hbm, out_v,
    dec_ref, frq_ref, skip_ref, x_v, w_raw, w_v, r_own, r_sib, drive, enter, excl, packed, packed_sib, acc,
    plane_buf, depth_buf, lam_tab, pow_tab, dep_tab,
    s_sem, x_sem, w_sem, r_sem, rs_send, rs_recv, pl_send, pl_recv, dp_send, dp_recv, pk_send, pk_recv, ready_sem,
):
    me, core = lax.axis_index("seq"), lax.axis_index("state")
    spot, deep = lax.rem(me, PLANE), lax.div(me, PLANE)
    px, py = lax.rem(spot, 4), lax.div(spot, 4)

    def plane_peer(d):
        spot_to = lax.rem(py + d // 4, 4) * 4 + lax.rem(px + d % 4, 4)
        return (deep * PLANE + spot_to, core), spot_to

    def depth_peer(d):
        return ((deep + d) * PLANE + spot, core)

    sibling = (me, 1 - core)

    small = [
        pltpu.make_async_copy(src, dst, s_sem.at[n])
        for n, (src, dst) in enumerate(((dec_hbm, dec_ref), (frq_hbm, frq_ref), (skip_hbm, skip_ref)))
    ]
    for cp in small:
        cp.start()
    x_cps = [
        pltpu.make_async_copy(x_hbm.at[:, pl.ds(KC * k, KC)], x_v.at[:, pl.ds(KC * k, KC)], x_sem.at[k])
        for k in range(KN)
    ]
    w_cps = [
        [
            pltpu.make_async_copy(w_hbm.at[pl.ds(KC * k, KC), :, pl.ds(GP * g, GP)], w_raw.at[g, k], w_sem.at[g, k])
            for k in range(KN)
        ]
        for g in range(GROUPS)
    ]

    def bring(n):
        if n < KN * GROUPS:
            g, k = divmod(n, KN)
            w_cps[g][k].start()
            if g == 0:
                x_cps[k].start()
        elif n == KN * GROUPS:
            for cp in r_cps:
                cp.start()

    for n in range(AHEAD):
        bring(n)
    my_cols = pl.multiple_of(core * COLS, COLS)
    sib_cols = pl.multiple_of((1 - core) * COLS, COLS)
    r_cps = [
        pltpu.make_async_copy(
            r_hbm.at[c, pl.ds(GP * g, GP), pl.ds(my_cols, COLS)], r_own.at[g, pl.ds(GP * c, GP)], r_sem.at[g, c]
        )
        for g in range(GROUPS)
        for c in range(2)
    ]

    barrier = pltpu.get_barrier_semaphore()
    for d in PLANE_ORDER:
        pl.semaphore_signal(barrier, inc=1, device_id=plane_peer(d)[0], device_id_type=MESH_ID)
    pl.semaphore_signal(barrier, inc=1, device_id=sibling, device_id_type=MESH_ID)

    def after(d, act):
        pl.when(deep + d < DEPTH)(act)

    def before(d, act):
        pl.when(deep - d >= 0)(act)

    def greet(d):
        pl.semaphore_signal(barrier, inc=1, device_id=depth_peer(d), device_id_type=MESH_ID)

    def answer(d):
        pl.semaphore_signal(ready_sem, inc=1, device_id=depth_peer(-d), device_id_type=MESH_ID)

    for d in DEPTH_ORDER:
        after(d, functools.partial(greet, d))

    depth_buf[...] = jnp.zeros_like(depth_buf)
    for cp in small:
        cp.wait()
    dec, frq = dec_ref[...], frq_ref[...]
    mod = jnp.exp(-dec)
    sq = dec * dec
    sinh = dec * (1.0 + sq / 6.0 * (1.0 + sq / 20.0 * (1.0 + sq / 42.0 * (1.0 + sq / 72.0))))
    gam = jnp.sqrt(2.0 * mod * sinh)
    base = (mod * jnp.cos(frq), mod * jnp.sin(frq))
    powers = [None, base]
    for n in range(2, SUB + 1):
        half = powers[n // 2]
        full = cmul(*half, *half)
        powers.append(cmul(*full, *base) if n % 2 else full)
    for n in range(SUB):
        pow_tab[0, pl.ds(n, 1), :] = powers[n + 1][0]
        pow_tab[1, pl.ds(n, 1), :] = powers[n + 1][1]
    one = (jnp.ones_like(dec), jnp.zeros_like(dec))
    subs = [one, powers[SUB]]
    for n in range(2, 9):
        subs.append(cmul(*subs[n // 2], *subs[n - n // 2]))
    sub_re = jnp.concatenate([p[0] for p in subs[:8]], axis=0)
    sub_im = jnp.concatenate([p[1] for p in subs[:8]], axis=0)
    lams = [one, subs[8]]
    for n in range(2, PLANE + 1):
        lams.append(cmul(*lams[n // 2], *lams[n - n // 2]))
    for n in range(PLANE):
        lam_tab[0, pl.ds(n, 1), :] = lams[n][0]
        lam_tab[1, pl.ds(n, 1), :] = lams[n][1]
    lead = lams[PLANE]
    here = (lam_tab[0, pl.ds(spot, 1), :], lam_tab[1, pl.ds(spot, 1), :])
    weight = (jnp.zeros_like(dec), jnp.zeros_like(dec))
    for n in range(DEPTH - 1, -1, -1):
        longer = cmul(*weight, *lead)
        first = deep - 1 == n
        weight = tuple(jnp.where(first, h, w) for h, w in zip(here, longer))
        dep_tab[0, pl.ds(n, 1), :] = weight[0]
        dep_tab[1, pl.ds(n, 1), :] = weight[1]

    step_of = lax.rem(lax.broadcasted_iota(jnp.int32, (CHUNKS, GP), 0), 8)
    sign = jnp.where(lax.broadcasted_iota(jnp.int32, (8, GP), 0) < 4, -1.0, 1.0)

    def weighted(parts, tab, order, lanes):
        along = jnp.zeros((8, GP), F32)
        across = jnp.zeros((8, GP), F32)
        for n, part in enumerate(parts):
            along = along + tab[0, pl.ds(order[n], 1), lanes] * part
            across = across + tab[1, pl.ds(order[n], 1), lanes] * part
        return along + sign * pltpu.roll(across, 4, 0)

    plane_cps, depth_cps, pack_cps, rs_cps = [[] for _ in range(GROUPS)], [[] for _ in range(GROUPS)], [], []

    def turn(g, k):
        for at in range(0, KC, 16):
            both = jnp.swapaxes(w_raw[g, k, pl.ds(at, 16)], 0, 1)
            w_v[g, pl.ds(KC * k + at, 16), pl.ds(0, GP)] = both[0]
            w_v[g, pl.ds(KC * k + at, 16), pl.ds(GP, GP)] = both[1]

    def fetch(g, k):
        w_cps[g][k].wait()
        if g == 0:
            x_cps[k].wait()
        bring(KN * g + k + AHEAD)
        turn(g, k)

    todo = [(g, n) for g in range(GROUPS) for n in range(KN)]
    fetch(*todo[0])
    for at, (g, n) in enumerate(todo):
        lanes = pl.ds(GP * g, GP)
        if at + 1 < len(todo):
            fetch(*todo[at + 1])
        deep_part = pl.ds(KC * n, KC)
        driven = jnp.dot(x_v[:, deep_part], w_v[g, deep_part, :], preferred_element_type=F32)
        for t in range(2 * GT):
            tile = driven[:, LANES * t : LANES * (t + 1)]
            for q in range(CHUNKS):
                rows, piece = pl.ds(PITCH * q, SUB), tile[SUB * q : SUB * (q + 1)]
                drive[g, t, rows, :] = piece if n == 0 else drive[g, t, rows, :] + piece
        if n + 1 < KN:
            continue

        lr, li = base[0][:, GP * g : GP * (g + 1)], base[1][:, GP * g : GP * (g + 1)]
        gg = gam[:, GP * g : GP * (g + 1)]
        sr = jnp.zeros((CHUNKS, GP), F32)
        si = jnp.zeros((CHUNKS, GP), F32)
        for i in range(SUB):
            tiles = [drive[g, t, pl.ds(i, CHUNKS, stride=PITCH), :] for t in range(2 * GT)]
            nr = lr * sr - li * si + gg * jnp.concatenate(tiles[:GT], axis=1)
            ni = lr * si + li * sr + gg * jnp.concatenate(tiles[GT:], axis=1)
            sr, si = nr, ni
            for t in range(GT):
                drive[g, t, pl.ds(i, CHUNKS, stride=PITCH), :] = sr[:, LANES * t : LANES * (t + 1)]
                drive[g, GT + t, pl.ds(i, CHUNKS, stride=PITCH), :] = si[:, LANES * t : LANES * (t + 1)]
        for d in (1, 2, 4):
            mr = jnp.where(step_of >= d, subs[d][0][:, GP * g : GP * (g + 1)], 0.0)
            mi = jnp.where(step_of >= d, subs[d][1][:, GP * g : GP * (g + 1)], 0.0)
            tr, ti = pltpu.roll(sr, d, 0), pltpu.roll(si, d, 0)
            sr, si = sr + mr * tr - mi * ti, si + mr * ti + mi * tr
        last = [v[8 * s + 7 : 8 * s + 8] for v in (sr, si) for s in range(SEQS)]
        last = jnp.concatenate(last, axis=0)
        tiles = [last[:, LANES * t : LANES * (t + 1)] for t in range(GT)]
        plane_buf[g, spot] = jnp.concatenate(tiles, axis=0)
        excl[g, 0] = jnp.where(step_of >= 1, pltpu.roll(sr, 1, 0), 0.0)
        excl[g, 1] = jnp.where(step_of >= 1, pltpu.roll(si, 1, 0), 0.0)

        if g == 0:
            pl.semaphore_wait(barrier, PLANE + deep)
            for d in DEPTH_ORDER:
                before(d, functools.partial(answer, d))
        for d in PLANE_ORDER:
            cp = pltpu.make_async_remote_copy(
                src_ref=plane_buf.at[g, spot], dst_ref=plane_buf.at[g, spot], send_sem=pl_send.at[g, d],
                recv_sem=pl_recv.at[g, d], device_id=plane_peer(d)[0], device_id_type=MESH_ID,
            )
            cp.start()
            plane_cps[g].append(cp)
        if g == GROUPS - 1:
            for h in range(GROUPS):
                for c in range(2):
                    cp = pltpu.make_async_remote_copy(
                        src_ref=r_hbm.at[c, pl.ds(GP * h, GP), pl.ds(sib_cols, COLS)],
                        dst_ref=r_sib.at[h, pl.ds(GP * c, GP)], send_sem=rs_send.at[h, c],
                        recv_sem=rs_recv.at[h, c], device_id=sibling, device_id_type=MESH_ID,
                    )
                    cp.start()
                    rs_cps.append(cp)

    entering = []
    for g in range(GROUPS):
        lanes = pl.ds(GP * g, GP)
        for cp in plane_cps[g]:
            cp.wait_recv()
        parts = [plane_buf[g, n].astype(F32) for n in range(PLANE)]
        parts = [jnp.concatenate([p[8 * t : 8 * (t + 1)] for t in range(GT)], axis=1) for p in parts]
        depth_buf[g, deep] = weighted(parts, lam_tab, [PLANE - 1 - n for n in range(PLANE)], lanes)
        if g == 0:

            @pl.when(deep < DEPTH - 1)
            def _():
                pl.semaphore_wait(ready_sem, DEPTH - 1 - deep)

        for d in DEPTH_ORDER:
            cp = pltpu.make_async_remote_copy(
                src_ref=depth_buf.at[g, deep], dst_ref=depth_buf.at[g, deep], send_sem=dp_send.at[g, d],
                recv_sem=dp_recv.at[g, d], device_id=depth_peer(d), device_id_type=MESH_ID,
            )
            after(d, cp.start)
            depth_cps[g].append((d, cp))
        lam_re, lam_im = lam_tab[0, pl.ds(1, 1), lanes], lam_tab[1, pl.ds(1, 1), lanes] * sign
        pre = jnp.zeros((8, GP), F32)
        for n in range(PLANE - 1):
            longer = lam_re * pre + lam_im * pltpu.roll(pre, 4, 0) + parts[n]
            pre = jnp.where(n < spot, longer, pre)
        entering.append(pre)
    for cp in r_cps:
        cp.wait()
    for cp in rs_cps:
        cp.wait_recv()

    skip = skip_ref[...]
    for g in range(GROUPS):
        lanes = pl.ds(GP * g, GP)
        for d, cp in depth_cps[g]:
            before(d, cp.wait_recv)
        come = entering[g] + weighted([depth_buf[g, n] for n in range(DEPTH)], dep_tab, list(range(DEPTH)), lanes)
        cr = jnp.concatenate([jnp.broadcast_to(come[s : s + 1], (8, GP)) for s in range(SEQS)], axis=0)
        ci = jnp.concatenate([jnp.broadcast_to(come[4 + s : 5 + s], (8, GP)) for s in range(SEQS)], axis=0)
        qr = jnp.concatenate([sub_re[:, GP * g : GP * (g + 1)]] * SEQS, axis=0)
        qi = jnp.concatenate([sub_im[:, GP * g : GP * (g + 1)]] * SEQS, axis=0)
        tr = excl[g, 0] + qr * cr - qi * ci
        ti = excl[g, 1] + qr * ci + qi * cr
        enter[g, 0], enter[g, 1] = tr, ti
        ar, ai = pow_tab[0, :, lanes], pow_tab[1, :, lanes]
        for h in range(HALVES):
            for q in range(CHUNKS // HALVES * h, CHUNKS // HALVES * (h + 1)):
                rows = pl.ds(SUB * q, SUB)
                br, bi = enter[g, 0, pl.ds(q, 1), :], enter[g, 1, pl.ds(q, 1), :]
                held = pl.ds(PITCH * q, SUB)
                er = jnp.concatenate([drive[g, t, held, :] for t in range(GT)], axis=1)
                ei = jnp.concatenate([drive[g, GT + t, held, :] for t in range(GT)], axis=1)
                packed[g, rows, pl.ds(0, GP)] = (er + ar * br - ai * bi).astype(BF16)
                packed[g, rows, pl.ds(GP, GP)] = (ei + ar * bi + ai * br).astype(BF16)
            rows = pl.ds(HALF * h, HALF)
            cp = pltpu.make_async_remote_copy(
                src_ref=packed.at[g, rows], dst_ref=packed_sib.at[g, rows], send_sem=pk_send.at[g, h],
                recv_sem=pk_recv.at[g, h], device_id=sibling, device_id_type=MESH_ID,
            )
            cp.start()
            pack_cps.append(cp)
        part = jnp.dot(packed[g], r_own[g], preferred_element_type=F32)
        if g == 0:
            straight = x_v[:, pl.ds(my_cols, COLS)].astype(F32) * skip
            acc[...] = part + straight
        else:
            acc[...] += part
        if g < GROUPS - 1:
            for cp in pack_cps[-HALVES:]:
                cp.wait_recv()
            acc[...] += jnp.dot(packed_sib[g], r_sib[g], preferred_element_type=F32)
    last = GROUPS - 1
    for h in range(HALVES):
        pack_cps[h - HALVES].wait_recv()
        rows = pl.ds(HALF * h, HALF)
        for c in range(COLS // CN):
            cols = pl.ds(CN * c, CN)
            part = jnp.dot(packed_sib[last, rows, :], r_sib[last, :, cols], preferred_element_type=F32)
            out_v[rows, cols] = (acc[rows, cols] + part).astype(BF16)
    for g in range(GROUPS):
        for cp in plane_cps[g]:
            cp.wait_send()
        for d, cp in depth_cps[g]:
            after(d, cp.wait_send)
    for cp in pack_cps + rs_cps:
        cp.wait_send()


def local(inputs, in_proj, decay_rate, frequency, readout, skip_gain):
    hbm = pl.BlockSpec(memory_space=pltpu.HBM)
    dma = pltpu.SemaphoreType.DMA
    out = pl.pallas_call(
        kernel,
        out_shape=pltpu.VMEM((ROWS, COLS), BF16),
        in_specs=[hbm] * 6,
        out_specs=pl.BlockSpec(memory_space=pltpu.VMEM),
        scratch_shapes=[
            pltpu.VMEM((1, POLES), F32),
            pltpu.VMEM((1, POLES), F32),
            pltpu.VMEM((1, COLS), F32),
            pltpu.VMEM((ROWS, WIDTH), BF16),
            pltpu.VMEM((GROUPS, KN, KC, 2, GP), BF16),
            pltpu.VMEM((GROUPS, WIDTH, 2 * GP), BF16),
            pltpu.VMEM((GROUPS, 2 * GP, COLS), BF16),
            pltpu.VMEM((GROUPS, 2 * GP, COLS), BF16),
            pltpu.VMEM((GROUPS, 2 * GT, CHUNKS * PITCH + SUB, LANES), F32),
            pltpu.VMEM((GROUPS, 2, CHUNKS, GP), F32),
            pltpu.VMEM((GROUPS, 2, CHUNKS, GP), F32),
            pltpu.VMEM((GROUPS, ROWS, 2 * GP), BF16),
            pltpu.VMEM((GROUPS, ROWS, 2 * GP), BF16),
            pltpu.VMEM((ROWS, COLS), F32),
            pltpu.VMEM((GROUPS, PLANE, 8 * GT, LANES), F32),
            pltpu.VMEM((GROUPS, DEPTH, 8, GP), F32),
            pltpu.VMEM((2, PLANE, POLES), F32),
            pltpu.VMEM((2, SUB, POLES), F32),
            pltpu.VMEM((2, DEPTH, POLES), F32),
            dma((3,)),
            dma((KN,)),
            dma((GROUPS, KN)),
            dma((GROUPS, 2)),
            dma((GROUPS, 2)),
            dma((GROUPS, 2)),
            dma((GROUPS, PLANE)),
            dma((GROUPS, PLANE)),
            dma((GROUPS, DEPTH)),
            dma((GROUPS, DEPTH)),
            dma((GROUPS, HALVES)),
            dma((GROUPS, HALVES)),
            pltpu.SemaphoreType.REGULAR,
        ],
        compiler_params=pltpu.CompilerParams(
            collective_id=0, has_side_effects=True, vmem_limit_bytes=40 << 20
        ),
    )(
        *[
            pltpu.with_memory_space_constraint(part, pltpu.HBM)
            for part in (
                inputs.reshape(ROWS, WIDTH), in_proj, decay_rate.reshape(1, POLES), frequency.reshape(1, POLES),
                readout, skip_gain.reshape(1, COLS),
            )
        ]
    )
    return out.reshape(SEQS, STEPS, COLS)


def solution(mesh):
    in_specs = (
        P(None, "seq", None),
        P(None, None, "state"),
        P("state"),
        P("state"),
        P(None, "state", None),
        P("state"),
    )
    out_specs = P(None, "seq", "state")
    return jax.shard_map(local, mesh=mesh, in_specs=in_specs, out_specs=out_specs, check_vma=False)
```

```python
import functools

import jax
import jax.numpy as jnp
from jax import lax
from jax.experimental import pallas as pl
from jax.experimental.pallas import tpu as pltpu
from jax.sharding import PartitionSpec as P

F32 = jnp.float32
BF16 = jnp.bfloat16
MESH_ID = pl.DeviceIdType.MESH

SEQS = 4
STEPS = 128
ROWS = SEQS * STEPS
WIDTH = 2048
POLES = 512
GROUPS = 1
GP = POLES // GROUPS
SUB = 16
CHUNKS = ROWS // SUB
KC = 256
KN = WIDTH // KC
AHEAD = 4
PITCH = 17
COLS = 1024
LANES = 128
GT = GP // LANES
HALVES = 4
PIECES = 4
HALF = ROWS // HALVES
CN = 256
PLANE = 16
DEPTH = 8
PLANE_ORDER = sorted(range(1, PLANE), key=lambda d: -(min(d % 4, 4 - d % 4) + min(d // 4, 4 - d // 4)))
DEPTH_ORDER = sorted(range(1, DEPTH), key=lambda d: -min(d, DEPTH - d))


def cmul(ar, ai, br, bi):
    return ar * br - ai * bi, ar * bi + ai * br


def kernel(
    x_hbm, w_hbm, dec_hbm, frq_hbm, r_hbm, skip_hbm, out_v,
    dec_ref, frq_ref, skip_ref, x_v, w_raw, w_v, r_own, r_sib, drive, enter, excl, packed, packed_sib, acc,
    plane_buf, depth_buf, lam_tab, pow_tab, dep_tab, pre_tab,
    s_sem, x_sem, w_sem, r_sem, rs_send, rs_recv, pl_send, pl_recv, dp_send, dp_recv, pk_send, pk_recv, ready_sem,
):
    me, core = lax.axis_index("seq"), lax.axis_index("state")
    spot, deep = lax.rem(me, PLANE), lax.div(me, PLANE)
    px, py = lax.rem(spot, 4), lax.div(spot, 4)

    def plane_peer(d):
        spot_to = lax.rem(py + d // 4, 4) * 4 + lax.rem(px + d % 4, 4)
        return (deep * PLANE + spot_to, core), spot_to

    def depth_peer(d):
        return ((deep + d) * PLANE + spot, core)

    sibling = (me, 1 - core)

    small = [
        pltpu.make_async_copy(src, dst, s_sem.at[n])
        for n, (src, dst) in enumerate(((dec_hbm, dec_ref), (frq_hbm, frq_ref), (skip_hbm, skip_ref)))
    ]
    for cp in small:
        cp.start()
    x_cps = [
        pltpu.make_async_copy(x_hbm.at[:, pl.ds(KC * k, KC)], x_v.at[:, pl.ds(KC * k, KC)], x_sem.at[k])
        for k in range(KN)
    ]
    w_cps = [
        [
            pltpu.make_async_copy(w_hbm.at[pl.ds(KC * k, KC), :, pl.ds(GP * g, GP)], w_raw.at[g, k], w_sem.at[g, k])
            for k in range(KN)
        ]
        for g in range(GROUPS)
    ]

    def bring(n):
        if n < KN * GROUPS:
            g, k = divmod(n, KN)
            w_cps[g][k].start()
            if g == 0:
                x_cps[k].start()
        elif n == KN * GROUPS:
            for cp in r_cps:
                cp.start()

    for n in range(AHEAD):
        bring(n)
    my_cols = pl.multiple_of(core * COLS, COLS)
    sib_cols = pl.multiple_of((1 - core) * COLS, COLS)
    r_cps = [
        pltpu.make_async_copy(
            r_hbm.at[c, pl.ds(GP * g, GP), pl.ds(my_cols, COLS)], r_own.at[g, pl.ds(GP * c, GP)], r_sem.at[g, c]
        )
        for g in range(GROUPS)
        for c in range(2)
    ]

    barrier = pltpu.get_barrier_semaphore()
    for d in PLANE_ORDER:
        pl.semaphore_signal(barrier, inc=1, device_id=plane_peer(d)[0], device_id_type=MESH_ID)
    pl.semaphore_signal(barrier, inc=1, device_id=sibling, device_id_type=MESH_ID)

    def after(d, act):
        pl.when(deep + d < DEPTH)(act)

    def before(d, act):
        pl.when(deep - d >= 0)(act)

    def greet(d):
        pl.semaphore_signal(barrier, inc=1, device_id=depth_peer(d), device_id_type=MESH_ID)

    def answer(d):
        pl.semaphore_signal(ready_sem, inc=1, device_id=depth_peer(-d), device_id_type=MESH_ID)

    for d in DEPTH_ORDER:
        after(d, functools.partial(greet, d))

    depth_buf[...] = jnp.zeros_like(depth_buf)
    for cp in small:
        cp.wait()
    dec, frq = dec_ref[...], frq_ref[...]
    mod = jnp.exp(-dec)
    sq = dec * dec
    sinh = dec * (1.0 + sq / 6.0 * (1.0 + sq / 20.0 * (1.0 + sq / 42.0 * (1.0 + sq / 72.0))))
    gam = jnp.sqrt(2.0 * mod * sinh)
    base = (mod * jnp.cos(frq), mod * jnp.sin(frq))
    powers = [None, base]
    for n in range(2, SUB + 1):
        half = powers[n // 2]
        full = cmul(*half, *half)
        powers.append(cmul(*full, *base) if n % 2 else full)
    for n in range(SUB):
        pow_tab[0, pl.ds(n, 1), :] = powers[n + 1][0]
        pow_tab[1, pl.ds(n, 1), :] = powers[n + 1][1]
    one = (jnp.ones_like(dec), jnp.zeros_like(dec))
    subs = [one, powers[SUB]]
    for n in range(2, 9):
        subs.append(cmul(*subs[n // 2], *subs[n - n // 2]))
    sub_re = jnp.concatenate([p[0] for p in subs[:8]], axis=0)
    sub_im = jnp.concatenate([p[1] for p in subs[:8]], axis=0)
    lams = [one, subs[8]]
    for n in range(2, PLANE + 1):
        lams.append(cmul(*lams[n // 2], *lams[n - n // 2]))
    for n in range(PLANE):
        lam_tab[0, pl.ds(n, 1), :] = lams[n][0]
        lam_tab[1, pl.ds(n, 1), :] = lams[n][1]
    lead = lams[PLANE]
    here = (lam_tab[0, pl.ds(spot, 1), :], lam_tab[1, pl.ds(spot, 1), :])
    weight = (jnp.zeros_like(dec), jnp.zeros_like(dec))
    for n in range(DEPTH - 1, -1, -1):
        longer = cmul(*weight, *lead)
        first = deep - 1 == n
        weight = tuple(jnp.where(first, h, w) for h, w in zip(here, longer))
        dep_tab[0, pl.ds(n, 1), :] = weight[0]
        dep_tab[1, pl.ds(n, 1), :] = weight[1]

    weight = (jnp.zeros_like(dec), jnp.zeros_like(dec))
    for n in range(PLANE - 1, -1, -1):
        longer = cmul(*weight, *lams[1])
        first = spot - 1 == n
        weight = tuple(jnp.where(first, h, w) for h, w in zip(one, longer))
        pre_tab[0, pl.ds(n, 1), :] = weight[0]
        pre_tab[1, pl.ds(n, 1), :] = weight[1]

    step_of = lax.rem(lax.broadcasted_iota(jnp.int32, (CHUNKS, GP), 0), 8)
    sign = jnp.where(lax.broadcasted_iota(jnp.int32, (8, GP), 0) < 4, -1.0, 1.0)

    def weighted(parts, tab, order, lanes):
        along = jnp.zeros((8, GP), F32)
        across = jnp.zeros((8, GP), F32)
        for n, part in enumerate(parts):
            along = along + tab[0, pl.ds(order[n], 1), lanes] * part
            across = across + tab[1, pl.ds(order[n], 1), lanes] * part
        return along + sign * pltpu.roll(across, 4, 0)

    plane_cps, depth_cps, pack_cps, rs_cps = [[] for _ in range(GROUPS)], [[] for _ in range(GROUPS)], [], []

    def turn(g, k):
        for at in range(0, KC, 16):
            both = jnp.swapaxes(w_raw[g, k, pl.ds(at, 16)], 0, 1)
            w_v[g, pl.ds(KC * k + at, 16), pl.ds(0, GP)] = both[0]
            w_v[g, pl.ds(KC * k + at, 16), pl.ds(GP, GP)] = both[1]

    def fetch(g, k):
        w_cps[g][k].wait()
        if g == 0:
            x_cps[k].wait()
        bring(KN * g + k + AHEAD)
        turn(g, k)

    todo = [(g, n) for g in range(GROUPS) for n in range(KN)]
    fetch(*todo[0])
    for at, (g, n) in enumerate(todo):
        lanes = pl.ds(GP * g, GP)
        if at + 1 < len(todo):
            fetch(*todo[at + 1])
        if g == 0 and n == KN - 2:
            pl.semaphore_wait(barrier, PLANE + deep)
            for d in DEPTH_ORDER:
                before(d, functools.partial(answer, d))
        deep_part = pl.ds(KC * n, KC)
        driven = jnp.dot(x_v[:, deep_part], w_v[g, deep_part, :], preferred_element_type=F32)
        for t in range(2 * GT):
            tile = driven[:, LANES * t : LANES * (t + 1)]
            for q in range(CHUNKS):
                rows, piece = pl.ds(PITCH * q, SUB), tile[SUB * q : SUB * (q + 1)]
                drive[g, t, rows, :] = piece if n == 0 else drive[g, t, rows, :] + piece
        if n + 1 < KN:
            continue

        lr, li = base[0][:, GP * g : GP * (g + 1)], base[1][:, GP * g : GP * (g + 1)]
        gg = gam[:, GP * g : GP * (g + 1)]
        sr = jnp.zeros((CHUNKS, GP), F32)
        si = jnp.zeros((CHUNKS, GP), F32)
        for i in range(SUB):
            tiles = [drive[g, t, pl.ds(i, CHUNKS, stride=PITCH), :] for t in range(2 * GT)]
            nr = lr * sr - li * si + gg * jnp.concatenate(tiles[:GT], axis=1)
            ni = lr * si + li * sr + gg * jnp.concatenate(tiles[GT:], axis=1)
            sr, si = nr, ni
            for t in range(GT):
                drive[g, t, pl.ds(i, CHUNKS, stride=PITCH), :] = sr[:, LANES * t : LANES * (t + 1)]
                drive[g, GT + t, pl.ds(i, CHUNKS, stride=PITCH), :] = si[:, LANES * t : LANES * (t + 1)]
        for d in (1, 2, 4):
            mr = jnp.where(step_of >= d, subs[d][0][:, GP * g : GP * (g + 1)], 0.0)
            mi = jnp.where(step_of >= d, subs[d][1][:, GP * g : GP * (g + 1)], 0.0)
            tr, ti = pltpu.roll(sr, d, 0), pltpu.roll(si, d, 0)
            sr, si = sr + mr * tr - mi * ti, si + mr * ti + mi * tr
        last = [v[8 * s + 7 : 8 * s + 8] for v in (sr, si) for s in range(SEQS)]
        last = jnp.concatenate(last, axis=0)
        tiles = [last[:, LANES * t : LANES * (t + 1)] for t in range(GT)]
        plane_buf[g, spot] = jnp.concatenate(tiles, axis=0)
        excl[g, 0] = jnp.where(step_of >= 1, pltpu.roll(sr, 1, 0), 0.0)
        excl[g, 1] = jnp.where(step_of >= 1, pltpu.roll(si, 1, 0), 0.0)

        for d in PLANE_ORDER:
            cp = pltpu.make_async_remote_copy(
                src_ref=plane_buf.at[g, spot], dst_ref=plane_buf.at[g, spot], send_sem=pl_send.at[g, d],
                recv_sem=pl_recv.at[g, d], device_id=plane_peer(d)[0], device_id_type=MESH_ID,
            )
            cp.start()
            plane_cps[g].append(cp)
    for h in range(GROUPS):
        for c in range(2):
            cp = pltpu.make_async_remote_copy(
                src_ref=r_hbm.at[c, pl.ds(GP * h, GP), pl.ds(sib_cols, COLS)],
                dst_ref=r_sib.at[h, pl.ds(GP * c, GP)], send_sem=rs_send.at[h, c],
                recv_sem=rs_recv.at[h, c], device_id=sibling, device_id_type=MESH_ID,
            )
            cp.start()
            rs_cps.append(cp)

    entering = []
    for g in range(GROUPS):
        lanes = pl.ds(GP * g, GP)
        for cp in plane_cps[g]:
            cp.wait_recv()
        parts = [plane_buf[g, n].astype(F32) for n in range(PLANE)]
        parts = [jnp.concatenate([p[8 * t : 8 * (t + 1)] for t in range(GT)], axis=1) for p in parts]
        depth_buf[g, deep] = weighted(parts, lam_tab, [PLANE - 1 - n for n in range(PLANE)], lanes)
        if g == 0:

            @pl.when(deep < DEPTH - 1)
            def _():
                pl.semaphore_wait(ready_sem, DEPTH - 1 - deep)

        for d in DEPTH_ORDER:
            cp = pltpu.make_async_remote_copy(
                src_ref=depth_buf.at[g, deep], dst_ref=depth_buf.at[g, deep], send_sem=dp_send.at[g, d],
                recv_sem=dp_recv.at[g, d], device_id=depth_peer(d), device_id_type=MESH_ID,
            )
            after(d, cp.start)
            depth_cps[g].append((d, cp))
        entering.append(weighted(parts, pre_tab, list(range(PLANE)), lanes))
    for cp in r_cps:
        cp.wait()
    acc[...] = x_v[:, pl.ds(my_cols, COLS)].astype(F32) * skip_ref[...]
    for g in range(GROUPS):
        lanes = pl.ds(GP * g, GP)
        for d, cp in depth_cps[g]:
            before(d, cp.wait_recv)
        come = entering[g] + weighted([depth_buf[g, n] for n in range(DEPTH)], dep_tab, list(range(DEPTH)), lanes)
        cr = jnp.concatenate([jnp.broadcast_to(come[s : s + 1], (8, GP)) for s in range(SEQS)], axis=0)
        ci = jnp.concatenate([jnp.broadcast_to(come[4 + s : 5 + s], (8, GP)) for s in range(SEQS)], axis=0)
        qr = jnp.concatenate([sub_re[:, GP * g : GP * (g + 1)]] * SEQS, axis=0)
        qi = jnp.concatenate([sub_im[:, GP * g : GP * (g + 1)]] * SEQS, axis=0)
        tr = excl[g, 0] + qr * cr - qi * ci
        ti = excl[g, 1] + qr * ci + qi * cr
        enter[g, 0], enter[g, 1] = tr, ti
        ar, ai = pow_tab[0, :, lanes], pow_tab[1, :, lanes]
        for h in range(PIECES):
            for q in range(CHUNKS // PIECES * h, CHUNKS // PIECES * (h + 1)):
                rows = pl.ds(SUB * q, SUB)
                br, bi = enter[g, 0, pl.ds(q, 1), :], enter[g, 1, pl.ds(q, 1), :]
                held = pl.ds(PITCH * q, SUB)
                er = jnp.concatenate([drive[g, t, held, :] for t in range(GT)], axis=1)
                ei = jnp.concatenate([drive[g, GT + t, held, :] for t in range(GT)], axis=1)
                packed[g, rows, pl.ds(0, GP)] = (er + ar * br - ai * bi).astype(BF16)
                packed[g, rows, pl.ds(GP, GP)] = (ei + ar * bi + ai * br).astype(BF16)
            rows = pl.ds(ROWS // PIECES * h, ROWS // PIECES)
            cp = pltpu.make_async_remote_copy(
                src_ref=packed.at[g, rows], dst_ref=packed_sib.at[g, rows], send_sem=pk_send.at[g, h],
                recv_sem=pk_recv.at[g, h], device_id=sibling, device_id_type=MESH_ID,
            )
            cp.start()
            pack_cps.append(cp)
        part = jnp.dot(packed[g], r_own[g], preferred_element_type=F32)
        acc[...] += part
        if g == 0:
            for cp in rs_cps:
                cp.wait_recv()
        if g < GROUPS - 1:
            for cp in pack_cps[-PIECES:]:
                cp.wait_recv()
            acc[...] += jnp.dot(packed_sib[g], r_sib[g], preferred_element_type=F32)
    last = GROUPS - 1
    for h in range(HALVES):
        for n in range(PIECES // HALVES):
            pack_cps[PIECES // HALVES * h + n - PIECES].wait_recv()
        rows = pl.ds(HALF * h, HALF)
        for c in range(COLS // CN):
            cols = pl.ds(CN * c, CN)
            part = jnp.dot(packed_sib[last, rows, :], r_sib[last, :, cols], preferred_element_type=F32)
            out_v[rows, cols] = (acc[rows, cols] + part).astype(BF16)
    for g in range(GROUPS):
        for cp in plane_cps[g]:
            cp.wait_send()
        for d, cp in depth_cps[g]:
            after(d, cp.wait_send)
    for cp in pack_cps + rs_cps:
        cp.wait_send()


def local(inputs, in_proj, decay_rate, frequency, readout, skip_gain):
    hbm = pl.BlockSpec(memory_space=pltpu.HBM)
    dma = pltpu.SemaphoreType.DMA
    out = pl.pallas_call(
        kernel,
        out_shape=pltpu.VMEM((ROWS, COLS), BF16),
        in_specs=[hbm] * 6,
        out_specs=pl.BlockSpec(memory_space=pltpu.VMEM),
        scratch_shapes=[
            pltpu.VMEM((1, POLES), F32),
            pltpu.VMEM((1, POLES), F32),
            pltpu.VMEM((1, COLS), F32),
            pltpu.VMEM((ROWS, WIDTH), BF16),
            pltpu.VMEM((GROUPS, KN, KC, 2, GP), BF16),
            pltpu.VMEM((GROUPS, WIDTH, 2 * GP), BF16),
            pltpu.VMEM((GROUPS, 2 * GP, COLS), BF16),
            pltpu.VMEM((GROUPS, 2 * GP, COLS), BF16),
            pltpu.VMEM((GROUPS, 2 * GT, CHUNKS * PITCH + SUB, LANES), F32),
            pltpu.VMEM((GROUPS, 2, CHUNKS, GP), F32),
            pltpu.VMEM((GROUPS, 2, CHUNKS, GP), F32),
            pltpu.VMEM((GROUPS, ROWS, 2 * GP), BF16),
            pltpu.VMEM((GROUPS, ROWS, 2 * GP), BF16),
            pltpu.VMEM((ROWS, COLS), F32),
            pltpu.VMEM((GROUPS, PLANE, 8 * GT, LANES), F32),
            pltpu.VMEM((GROUPS, DEPTH, 8, GP), F32),
            pltpu.VMEM((2, PLANE, POLES), F32),
            pltpu.VMEM((2, SUB, POLES), F32),
            pltpu.VMEM((2, DEPTH, POLES), F32),
            pltpu.VMEM((2, PLANE, POLES), F32),
            dma((3,)),
            dma((KN,)),
            dma((GROUPS, KN)),
            dma((GROUPS, 2)),
            dma((GROUPS, 2)),
            dma((GROUPS, 2)),
            dma((GROUPS, PLANE)),
            dma((GROUPS, PLANE)),
            dma((GROUPS, DEPTH)),
            dma((GROUPS, DEPTH)),
            dma((GROUPS, PIECES)),
            dma((GROUPS, PIECES)),
            pltpu.SemaphoreType.REGULAR,
        ],
        compiler_params=pltpu.CompilerParams(
            collective_id=0, has_side_effects=True, vmem_limit_bytes=40 << 20
        ),
    )(
        *[
            pltpu.with_memory_space_constraint(part, pltpu.HBM)
            for part in (
                inputs.reshape(ROWS, WIDTH), in_proj, decay_rate.reshape(1, POLES), frequency.reshape(1, POLES),
                readout, skip_gain.reshape(1, COLS),
            )
        ]
    )
    return out.reshape(SEQS, STEPS, COLS)


def solution(mesh):
    in_specs = (
        P(None, "seq", None),
        P(None, None, "state"),
        P("state"),
        P("state"),
        P(None, "state", None),
        P("state"),
    )
    out_specs = P(None, "seq", "state")
    return jax.shard_map(local, mesh=mesh, in_specs=in_specs, out_specs=out_specs, check_vma=False)
```

```python
import functools

import jax
import jax.numpy as jnp
from jax import lax
from jax.experimental import pallas as pl
from jax.experimental.pallas import tpu as pltpu
from jax.sharding import PartitionSpec as P

F32 = jnp.float32
BF16 = jnp.bfloat16
MESH_ID = pl.DeviceIdType.MESH

SEQS = 4
STEPS = 128
ROWS = SEQS * STEPS
WIDTH = 2048
POLES = 512
GROUPS = 1
GP = POLES // GROUPS
SUB = 16
CHUNKS = ROWS // SUB
KC = 256
KN = WIDTH // KC
AHEAD = 4
PITCH = 17
COLS = 1024
LANES = 128
GT = GP // LANES
HALVES = 2
PIECES = 2
HALF = ROWS // HALVES
CN = 256
PLANE = 16
DEPTH = 8
PLANE_ORDER = sorted(range(1, PLANE), key=lambda d: -(min(d % 4, 4 - d % 4) + min(d // 4, 4 - d // 4)))
DEPTH_ORDER = sorted(range(1, DEPTH), key=lambda d: -min(d, DEPTH - d))


def cmul(ar, ai, br, bi):
    return ar * br - ai * bi, ar * bi + ai * br


def kernel(
    x_hbm, w_hbm, dec_hbm, frq_hbm, r_hbm, skip_hbm, out_v,
    dec_ref, frq_ref, skip_ref, x_v, w_raw, w_v, r_own, r_sib, drive, enter, excl, packed, packed_sib, acc,
    plane_buf, depth_buf, lam_tab, pow_tab, dep_tab, pre_tab,
    s_sem, x_sem, w_sem, r_sem, rs_send, rs_recv, pl_send, pl_recv, dp_send, dp_recv, pk_send, pk_recv, ready_sem,
):
    me, core = lax.axis_index("seq"), lax.axis_index("state")
    spot, deep = lax.rem(me, PLANE), lax.div(me, PLANE)
    px, py = lax.rem(spot, 4), lax.div(spot, 4)

    def plane_peer(d):
        spot_to = lax.rem(py + d // 4, 4) * 4 + lax.rem(px + d % 4, 4)
        return (deep * PLANE + spot_to, core), spot_to

    def depth_peer(d):
        return ((deep + d) * PLANE + spot, core)

    sibling = (me, 1 - core)

    small = [
        pltpu.make_async_copy(src, dst, s_sem.at[n])
        for n, (src, dst) in enumerate(((dec_hbm, dec_ref), (frq_hbm, frq_ref), (skip_hbm, skip_ref)))
    ]
    for cp in small:
        cp.start()
    x_cps = [
        pltpu.make_async_copy(x_hbm.at[:, pl.ds(KC * k, KC)], x_v.at[:, pl.ds(KC * k, KC)], x_sem.at[k])
        for k in range(KN)
    ]
    w_cps = [
        [
            pltpu.make_async_copy(w_hbm.at[pl.ds(KC * k, KC), :, pl.ds(GP * g, GP)], w_raw.at[g, k], w_sem.at[g, k])
            for k in range(KN)
        ]
        for g in range(GROUPS)
    ]

    def bring(n):
        if n < KN * GROUPS:
            g, k = divmod(n, KN)
            w_cps[g][k].start()
            if g == 0:
                x_cps[k].start()
        elif n == KN * GROUPS:
            for cp in r_cps:
                cp.start()

    for n in range(AHEAD):
        bring(n)
    my_cols = pl.multiple_of(core * COLS, COLS)
    sib_cols = pl.multiple_of((1 - core) * COLS, COLS)
    r_cps = [
        pltpu.make_async_copy(
            r_hbm.at[c, pl.ds(GP * g, GP), pl.ds(my_cols, COLS)], r_own.at[g, pl.ds(GP * c, GP)], r_sem.at[g, c]
        )
        for g in range(GROUPS)
        for c in range(2)
    ]

    barrier = pltpu.get_barrier_semaphore()
    for d in PLANE_ORDER:
        pl.semaphore_signal(barrier, inc=1, device_id=plane_peer(d)[0], device_id_type=MESH_ID)
    pl.semaphore_signal(barrier, inc=1, device_id=sibling, device_id_type=MESH_ID)

    def after(d, act):
        pl.when(deep + d < DEPTH)(act)

    def before(d, act):
        pl.when(deep - d >= 0)(act)

    def greet(d):
        pl.semaphore_signal(barrier, inc=1, device_id=depth_peer(d), device_id_type=MESH_ID)

    def answer(d):
        pl.semaphore_signal(ready_sem, inc=1, device_id=depth_peer(-d), device_id_type=MESH_ID)

    for d in DEPTH_ORDER:
        after(d, functools.partial(greet, d))

    depth_buf[...] = jnp.zeros_like(depth_buf)
    for cp in small:
        cp.wait()
    dec, frq = dec_ref[...], frq_ref[...]
    mod = jnp.exp(-dec)
    sq = dec * dec
    sinh = dec * (1.0 + sq / 6.0 * (1.0 + sq / 20.0 * (1.0 + sq / 42.0 * (1.0 + sq / 72.0))))
    gam = jnp.sqrt(2.0 * mod * sinh)
    base = (mod * jnp.cos(frq), mod * jnp.sin(frq))
    powers = [None, base]
    for n in range(2, SUB + 1):
        half = powers[n // 2]
        full = cmul(*half, *half)
        powers.append(cmul(*full, *base) if n % 2 else full)
    for n in range(SUB):
        pow_tab[0, pl.ds(n, 1), :] = powers[n + 1][0]
        pow_tab[1, pl.ds(n, 1), :] = powers[n + 1][1]
    one = (jnp.ones_like(dec), jnp.zeros_like(dec))
    subs = [one, powers[SUB]]
    for n in range(2, 9):
        subs.append(cmul(*subs[n // 2], *subs[n - n // 2]))
    sub_re = jnp.concatenate([p[0] for p in subs[:8]], axis=0)
    sub_im = jnp.concatenate([p[1] for p in subs[:8]], axis=0)
    lams = [one, subs[8]]
    for n in range(2, PLANE + 1):
        lams.append(cmul(*lams[n // 2], *lams[n - n // 2]))
    for n in range(PLANE):
        lam_tab[0, pl.ds(n, 1), :] = lams[n][0]
        lam_tab[1, pl.ds(n, 1), :] = lams[n][1]
    lead = lams[PLANE]
    here = (lam_tab[0, pl.ds(spot, 1), :], lam_tab[1, pl.ds(spot, 1), :])
    weight = (jnp.zeros_like(dec), jnp.zeros_like(dec))
    for n in range(DEPTH - 1, -1, -1):
        longer = cmul(*weight, *lead)
        first = deep - 1 == n
        weight = tuple(jnp.where(first, h, w) for h, w in zip(here, longer))
        dep_tab[0, pl.ds(n, 1), :] = weight[0]
        dep_tab[1, pl.ds(n, 1), :] = weight[1]

    weight = (jnp.zeros_like(dec), jnp.zeros_like(dec))
    for n in range(PLANE - 1, -1, -1):
        longer = cmul(*weight, *lams[1])
        first = spot - 1 == n
        weight = tuple(jnp.where(first, h, w) for h, w in zip(one, longer))
        pre_tab[0, pl.ds(n, 1), :] = weight[0]
        pre_tab[1, pl.ds(n, 1), :] = weight[1]

    step_of = lax.rem(lax.broadcasted_iota(jnp.int32, (CHUNKS, GP), 0), 8)
    sign = jnp.where(lax.broadcasted_iota(jnp.int32, (8, GP), 0) < 4, -1.0, 1.0)

    def weighted(parts, tab, order, lanes):
        along = jnp.zeros((8, GP), F32)
        across = jnp.zeros((8, GP), F32)
        for n, part in enumerate(parts):
            along = along + tab[0, pl.ds(order[n], 1), lanes] * part
            across = across + tab[1, pl.ds(order[n], 1), lanes] * part
        return along + sign * pltpu.roll(across, 4, 0)

    plane_cps, depth_cps, pack_cps, rs_cps = [[] for _ in range(GROUPS)], [[] for _ in range(GROUPS)], [], []

    def turn(g, k):
        for at in range(0, KC, 16):
            both = jnp.swapaxes(w_raw[g, k, pl.ds(at, 16)], 0, 1)
            w_v[g, pl.ds(KC * k + at, 16), pl.ds(0, GP)] = both[0]
            w_v[g, pl.ds(KC * k + at, 16), pl.ds(GP, GP)] = both[1]

    def fetch(g, k):
        w_cps[g][k].wait()
        if g == 0:
            x_cps[k].wait()
        bring(KN * g + k + AHEAD)
        turn(g, k)

    todo = [(g, n) for g in range(GROUPS) for n in range(KN)]
    fetch(*todo[0])
    for at, (g, n) in enumerate(todo):
        lanes = pl.ds(GP * g, GP)
        if at + 1 < len(todo):
            fetch(*todo[at + 1])
        deep_part = pl.ds(KC * n, KC)
        driven = jnp.dot(x_v[:, deep_part], w_v[g, deep_part, :], preferred_element_type=F32)
        for t in range(2 * GT):
            tile = driven[:, LANES * t : LANES * (t + 1)]
            for q in range(CHUNKS):
                rows, piece = pl.ds(PITCH * q, SUB), tile[SUB * q : SUB * (q + 1)]
                drive[g, t, rows, :] = piece if n == 0 else drive[g, t, rows, :] + piece
        if n + 1 < KN:
            continue

        lr, li = base[0][:, GP * g : GP * (g + 1)], base[1][:, GP * g : GP * (g + 1)]
        gg = gam[:, GP * g : GP * (g + 1)]
        sr = jnp.zeros((CHUNKS, GP), F32)
        si = jnp.zeros((CHUNKS, GP), F32)
        for i in range(SUB):
            tiles = [drive[g, t, pl.ds(i, CHUNKS, stride=PITCH), :] for t in range(2 * GT)]
            nr = lr * sr - li * si + gg * jnp.concatenate(tiles[:GT], axis=1)
            ni = lr * si + li * sr + gg * jnp.concatenate(tiles[GT:], axis=1)
            sr, si = nr, ni
            for t in range(GT):
                drive[g, t, pl.ds(i, CHUNKS, stride=PITCH), :] = sr[:, LANES * t : LANES * (t + 1)]
                drive[g, GT + t, pl.ds(i, CHUNKS, stride=PITCH), :] = si[:, LANES * t : LANES * (t + 1)]
        for d in (1, 2, 4):
            mr = jnp.where(step_of >= d, subs[d][0][:, GP * g : GP * (g + 1)], 0.0)
            mi = jnp.where(step_of >= d, subs[d][1][:, GP * g : GP * (g + 1)], 0.0)
            tr, ti = pltpu.roll(sr, d, 0), pltpu.roll(si, d, 0)
            sr, si = sr + mr * tr - mi * ti, si + mr * ti + mi * tr
        last = [v[8 * s + 7 : 8 * s + 8] for v in (sr, si) for s in range(SEQS)]
        last = jnp.concatenate(last, axis=0)
        tiles = [last[:, LANES * t : LANES * (t + 1)] for t in range(GT)]
        plane_buf[g, spot] = jnp.concatenate(tiles, axis=0)
        excl[g, 0] = jnp.where(step_of >= 1, pltpu.roll(sr, 1, 0), 0.0)
        excl[g, 1] = jnp.where(step_of >= 1, pltpu.roll(si, 1, 0), 0.0)

        if g == 0:
            pl.semaphore_wait(barrier, PLANE + deep)
            for d in DEPTH_ORDER:
                before(d, functools.partial(answer, d))
        for d in PLANE_ORDER:
            cp = pltpu.make_async_remote_copy(
                src_ref=plane_buf.at[g, spot], dst_ref=plane_buf.at[g, spot], send_sem=pl_send.at[g, d],
                recv_sem=pl_recv.at[g, d], device_id=plane_peer(d)[0], device_id_type=MESH_ID,
            )
            cp.start()
            plane_cps[g].append(cp)
    for h in range(GROUPS):
        for c in range(2):
            cp = pltpu.make_async_remote_copy(
                src_ref=r_hbm.at[c, pl.ds(GP * h, GP), pl.ds(sib_cols, COLS)],
                dst_ref=r_sib.at[h, pl.ds(GP * c, GP)], send_sem=rs_send.at[h, c],
                recv_sem=rs_recv.at[h, c], device_id=sibling, device_id_type=MESH_ID,
            )
            cp.start()
            rs_cps.append(cp)

    entering = []
    for g in range(GROUPS):
        lanes = pl.ds(GP * g, GP)
        for cp in plane_cps[g]:
            cp.wait_recv()
        parts = [plane_buf[g, n].astype(F32) for n in range(PLANE)]
        parts = [jnp.concatenate([p[8 * t : 8 * (t + 1)] for t in range(GT)], axis=1) for p in parts]
        depth_buf[g, deep] = weighted(parts, lam_tab, [PLANE - 1 - n for n in range(PLANE)], lanes)
        if g == 0:

            @pl.when(deep < DEPTH - 1)
            def _():
                pl.semaphore_wait(ready_sem, DEPTH - 1 - deep)

        for d in DEPTH_ORDER:
            cp = pltpu.make_async_remote_copy(
                src_ref=depth_buf.at[g, deep], dst_ref=depth_buf.at[g, deep], send_sem=dp_send.at[g, d],
                recv_sem=dp_recv.at[g, d], device_id=depth_peer(d), device_id_type=MESH_ID,
            )
            after(d, cp.start)
            depth_cps[g].append((d, cp))
        entering.append(weighted(parts, pre_tab, list(range(PLANE)), lanes))
    for cp in r_cps:
        cp.wait()
    acc[...] = x_v[:, pl.ds(my_cols, COLS)].astype(F32) * skip_ref[...]
    for g in range(GROUPS):
        lanes = pl.ds(GP * g, GP)
        for d, cp in depth_cps[g]:
            before(d, cp.wait_recv)
        come = entering[g] + weighted([depth_buf[g, n] for n in range(DEPTH)], dep_tab, list(range(DEPTH)), lanes)
        cr = jnp.concatenate([jnp.broadcast_to(come[s : s + 1], (8, GP)) for s in range(SEQS)], axis=0)
        ci = jnp.concatenate([jnp.broadcast_to(come[4 + s : 5 + s], (8, GP)) for s in range(SEQS)], axis=0)
        qr = jnp.concatenate([sub_re[:, GP * g : GP * (g + 1)]] * SEQS, axis=0)
        qi = jnp.concatenate([sub_im[:, GP * g : GP * (g + 1)]] * SEQS, axis=0)
        tr = excl[g, 0] + qr * cr - qi * ci
        ti = excl[g, 1] + qr * ci + qi * cr
        enter[g, 0], enter[g, 1] = tr, ti
        ar, ai = pow_tab[0, :, lanes], pow_tab[1, :, lanes]
        for h in range(PIECES):
            for q in range(CHUNKS // PIECES * h, CHUNKS // PIECES * (h + 1)):
                rows = pl.ds(SUB * q, SUB)
                br, bi = enter[g, 0, pl.ds(q, 1), :], enter[g, 1, pl.ds(q, 1), :]
                held = pl.ds(PITCH * q, SUB)
                er = jnp.concatenate([drive[g, t, held, :] for t in range(GT)], axis=1)
                ei = jnp.concatenate([drive[g, GT + t, held, :] for t in range(GT)], axis=1)
                packed[g, rows, pl.ds(0, GP)] = (er + ar * br - ai * bi).astype(BF16)
                packed[g, rows, pl.ds(GP, GP)] = (ei + ar * bi + ai * br).astype(BF16)
            rows = pl.ds(ROWS // PIECES * h, ROWS // PIECES)
            cp = pltpu.make_async_remote_copy(
                src_ref=packed.at[g, rows], dst_ref=packed_sib.at[g, rows], send_sem=pk_send.at[g, h],
                recv_sem=pk_recv.at[g, h], device_id=sibling, device_id_type=MESH_ID,
            )
            cp.start()
            pack_cps.append(cp)
        part = jnp.dot(packed[g], r_own[g], preferred_element_type=F32)
        acc[...] += part
        if g == 0:
            for cp in rs_cps:
                cp.wait_recv()
        if g < GROUPS - 1:
            for cp in pack_cps[-PIECES:]:
                cp.wait_recv()
            acc[...] += jnp.dot(packed_sib[g], r_sib[g], preferred_element_type=F32)
    last = GROUPS - 1
    for h in range(HALVES):
        for n in range(PIECES // HALVES):
            pack_cps[PIECES // HALVES * h + n - PIECES].wait_recv()
        rows = pl.ds(HALF * h, HALF)
        for c in range(COLS // CN):
            cols = pl.ds(CN * c, CN)
            part = jnp.dot(packed_sib[last, rows, :], r_sib[last, :, cols], preferred_element_type=F32)
            out_v[rows, cols] = (acc[rows, cols] + part).astype(BF16)
    for g in range(GROUPS):
        for cp in plane_cps[g]:
            cp.wait_send()
        for d, cp in depth_cps[g]:
            after(d, cp.wait_send)
    for cp in pack_cps + rs_cps:
        cp.wait_send()


def local(inputs, in_proj, decay_rate, frequency, readout, skip_gain):
    hbm = pl.BlockSpec(memory_space=pltpu.HBM)
    dma = pltpu.SemaphoreType.DMA
    out = pl.pallas_call(
        kernel,
        out_shape=pltpu.VMEM((ROWS, COLS), BF16),
        in_specs=[hbm] * 6,
        out_specs=pl.BlockSpec(memory_space=pltpu.VMEM),
        scratch_shapes=[
            pltpu.VMEM((1, POLES), F32),
            pltpu.VMEM((1, POLES), F32),
            pltpu.VMEM((1, COLS), F32),
            pltpu.VMEM((ROWS, WIDTH), BF16),
            pltpu.VMEM((GROUPS, KN, KC, 2, GP), BF16),
            pltpu.VMEM((GROUPS, WIDTH, 2 * GP), BF16),
            pltpu.VMEM((GROUPS, 2 * GP, COLS), BF16),
            pltpu.VMEM((GROUPS, 2 * GP, COLS), BF16),
            pltpu.VMEM((GROUPS, 2 * GT, CHUNKS * PITCH + SUB, LANES), F32),
            pltpu.VMEM((GROUPS, 2, CHUNKS, GP), F32),
            pltpu.VMEM((GROUPS, 2, CHUNKS, GP), F32),
            pltpu.VMEM((GROUPS, ROWS, 2 * GP), BF16),
            pltpu.VMEM((GROUPS, ROWS, 2 * GP), BF16),
            pltpu.VMEM((ROWS, COLS), F32),
            pltpu.VMEM((GROUPS, PLANE, 8 * GT, LANES), F32),
            pltpu.VMEM((GROUPS, DEPTH, 8, GP), F32),
            pltpu.VMEM((2, PLANE, POLES), F32),
            pltpu.VMEM((2, SUB, POLES), F32),
            pltpu.VMEM((2, DEPTH, POLES), F32),
            pltpu.VMEM((2, PLANE, POLES), F32),
            dma((3,)),
            dma((KN,)),
            dma((GROUPS, KN)),
            dma((GROUPS, 2)),
            dma((GROUPS, 2)),
            dma((GROUPS, 2)),
            dma((GROUPS, PLANE)),
            dma((GROUPS, PLANE)),
            dma((GROUPS, DEPTH)),
            dma((GROUPS, DEPTH)),
            dma((GROUPS, PIECES)),
            dma((GROUPS, PIECES)),
            pltpu.SemaphoreType.REGULAR,
        ],
        compiler_params=pltpu.CompilerParams(
            collective_id=0, has_side_effects=True, vmem_limit_bytes=40 << 20
        ),
    )(
        *[
            pltpu.with_memory_space_constraint(part, pltpu.HBM)
            for part in (
                inputs.reshape(ROWS, WIDTH), in_proj, decay_rate.reshape(1, POLES), frequency.reshape(1, POLES),
                readout, skip_gain.reshape(1, COLS),
            )
        ]
    )
    return out.reshape(SEQS, STEPS, COLS)


def solution(mesh):
    in_specs = (
        P(None, "seq", None),
        P(None, None, "state"),
        P("state"),
        P("state"),
        P(None, "state", None),
        P("state"),
    )
    out_specs = P(None, "seq", "state")
    return jax.shard_map(local, mesh=mesh, in_specs=in_specs, out_specs=out_specs, check_vma=False)
```
